32 devices in a mesh: freq: 4 (over z), row: 8 (over y, x, core).
Axes of the slice: x: 2, y: 2, z: 4, core: 2. Of those that a mesh axis runs over, the one named last changes fastest.
Arguments:
- vis_values: bfloat16 [4, 512, 2, 128], P('freq', 'row'), may hold values from -6 to 6
- kernel_u: bfloat16 [4, 512, 7, 128], P('freq', 'row'), may hold values from 0.049804688 to 1
- kernel_v: bfloat16 [4, 512, 7, 128], P('freq', 'row'), may hold values from 0.049804688 to 1
- offset_u: int32 [4, 512, 128], P('freq', 'row'), may hold values from 0 to 9
- offset_v: int32 [4, 512, 128], P('freq', 'row'), may hold values from 0 to 121
- block_owner: int32 [4, 512, 1], P('freq', 'row'), may hold values from 0 to 7; in each aligned block of 64 rows (0 to 63, 64 to 127, ..., all dimensions but the last counted through in order) at most 32 rows name the same one
- tile_slot: int32 [4, 512], P('freq', 'row'), may hold values from 0 to 1023
- channel_freq: float32 [4], P('freq'), may hold values from 0.856 to 1.712
Outputs:
- taylor: bfloat16 [3, 4096, 4096], P(None, 'freq', 'row')
The draws below stay inside these ranges and needn't reach their ends.
Inputs may be any that keep to these rules, and one draw needn't show every extreme that they name: `block_owner`: among the 64 blocks of one channel held by one index of row, at most 32 name the same owner, a bound that some block reaches.
All inputs are finite; a program needn't handle non-finite values.
Results may differ from the reference program's by a relative error of at most 0.024.
Values may be sent and summed in bfloat16 or wider, within the bound.
A program may use at most 128 MiB of HBM per device.

```python
import math
import jax
import jax.numpy as jnp
import numpy as np
from jax import lax

GRID = 4096
TU = 16
TV = 128
TAPS = 7
BV = 128
NBLK = 64
CHANNELS = 4
BLOCKS = 512
CAP = 32
TS = 1024
N_ROW = 8


def touch_ends(values, stream_key, smallest, high):
    longest = values.shape.index(max(values.shape))
    spots = []
    for shift in (0, 1):
        where = [jax.random.randint(jax.random.fold_in(stream_key, axis), (), 0, length) for axis, length in enumerate(values.shape)]
        where[longest] = (where[longest] + shift) % values.shape[longest]
        spots.append(tuple(where))
    return values.at[spots[0]].set(smallest).at[spots[1]].set(high)


def steps_of(stream_key, extent, cuts, smallest, top_value):
    factor_of = 1.0
    for dim, parts in cuts:
        steps = jax.random.uniform(jax.random.fold_in(jax.random.fold_in(stream_key, 6), dim), (parts,), jnp.float32, smallest / len(cuts), top_value / len(cuts))
        factor_of = factor_of * jnp.repeat(jnp.exp(steps), extent[dim] // parts).reshape((-1,) + (1,) * (len(extent) - 1 - dim))
    return factor_of


def deal_out(own_key, own, number, rows, number_of, top, bound, skew):
    ranking = jax.random.permutation(own_key, number_of)
    heavy_load, common = portions_of(number_of, rows * top, bound, skew, True), portions_of(number_of, rows * top, bound, skew, False)
    places = jnp.arange(number_of)

    def named(tallies, rotation):
        used = int((tallies > 0).sum())
        fixed = max(1, used // 4)
        passed = fixed + (places - fixed + rotation * (used - fixed)) % max(1, number_of - fixed)
        return jnp.zeros((number_of,), jnp.int32).at[ranking[jnp.where(places < fixed, places, passed)]].set(jnp.asarray(tallies, jnp.int32))

    tallies = jnp.where(number % 4 == 0, named(heavy_load, number // 4), named(common, number - number // 4 - 1))
    mixed = jax.random.permutation(jax.random.fold_in(own, 3), number_of)
    source_of, receiver = mixed[0:number_of // 2 * 2:2], mixed[1:number_of // 2 * 2:2]
    slack = jnp.minimum(tallies[source_of] - 1, bound - tallies[receiver]) // 2
    slack = jnp.where((source_of == ranking[0]) | (receiver == ranking[0]) | (tallies[receiver] == 0), 0, jnp.maximum(slack, 0))
    passed = jax.random.randint(jax.random.fold_in(own, 4), (number_of // 2,), 0, 1 << 20) % (slack + 1)
    tallies = tallies.at[source_of].add(-passed).at[receiver].add(passed)
    items = jnp.searchsorted(jnp.cumsum(tallies), jnp.arange(rows * top), side="right").astype(jnp.int32)
    grid = items.reshape(top, rows).T
    grid = grid[jax.random.permutation(jax.random.fold_in(own, 1), rows)]
    rotation = jax.random.randint(jax.random.fold_in(own, 2), (rows, 1), 0, top)
    return jnp.take_along_axis(grid, (jnp.arange(top)[None, :] + rotation) % top, axis=1)


def portions_of(number_of, total, reach, lean, full):
    weights = [(1 << 20) // math.isqrt(grade ** lean) + 1 for grade in range(1, number_of + 1)]
    largest = reach if full else min(reach, max(-(-total // number_of), total * weights[0] // sum(weights)))
    least = 1 if total - largest >= number_of - 1 else 0
    counts, surplus = [largest] + [least] * (number_of - 1), total - largest - least * (number_of - 1)
    while surplus > 0:
        candidates = [i for i in range(1, number_of) if counts[i] < largest] or [i for i in range(1, number_of) if counts[i] < reach]
        mass, remaining = sum([weights[i] for i in candidates]), surplus
        for i in candidates:
            extra = min(reach - counts[i], max(1, remaining * weights[i] // mass), surplus)
            counts[i] = counts[i] + extra
            surplus = surplus - extra
    return np.array(counts)


def bell_draw(own_key, extent, width, most, cuts=(), held_as=jnp.bfloat16):
    drawn = jax.random.normal(own_key, extent, jnp.float32) * width
    if len(cuts) > 0:
        drawn = steps_of(own_key, extent, cuts, -0.22, 0.18) * drawn
    return jnp.clip(drawn, min=-most, max=most).astype(held_as)


def setup_inputs(seed: int = 0) -> dict:
    key_of = jax.random.split(jax.random.key(seed), 9)
    vis_values = bell_draw(key_of[0], (CHANNELS, BLOCKS, 2, BV), 1.0, 6.0, ((0, 4), (1, 8)))
    kernel_u = jnp.clip(jnp.exp(math.log(1.0) - 2.9996462 * jax.random.uniform(key_of[1], (CHANNELS, BLOCKS, TAPS, BV), jnp.float32) ** steps_of(key_of[1], (CHANNELS, BLOCKS, TAPS, BV), ((0, 4), (1, 8)), -0.2, 0.2)), 0.049804688, 1.0).astype(jnp.bfloat16)
    kernel_v = jnp.clip(jnp.exp(math.log(1.0) - 2.9996462 * jax.random.uniform(key_of[2], (CHANNELS, BLOCKS, TAPS, BV), jnp.float32) ** steps_of(key_of[2], (CHANNELS, BLOCKS, TAPS, BV), ((0, 4), (1, 8)), -0.2, 0.2)), 0.049804688, 1.0).astype(jnp.bfloat16)
    offset_u = touch_ends(jax.random.randint(key_of[3], (CHANNELS, BLOCKS, BV), 0, TU - TAPS + 1), jax.random.fold_in(key_of[3], 1), 0, TU - TAPS).astype(jnp.int32)
    offset_v = touch_ends(jax.random.randint(key_of[4], (CHANNELS, BLOCKS, BV), 0, TV - TAPS + 1), jax.random.fold_in(key_of[4], 1), 0, TV - TAPS).astype(jnp.int32)
    block_owner_keys = jax.random.split(jax.random.fold_in(key_of[5], 1), CHANNELS * BLOCKS // NBLK)
    block_owner_turns = jax.random.permutation(jax.random.fold_in(key_of[5], 3), CHANNELS * BLOCKS // NBLK)
    block_owner = jax.vmap(lambda own, number: deal_out(jax.random.fold_in(key_of[5], 2), own, number, NBLK, N_ROW, 1, CAP, 2))(block_owner_keys, block_owner_turns).reshape((CHANNELS, BLOCKS, 1))
    tile_slot = touch_ends(jax.random.randint(key_of[6], (CHANNELS, BLOCKS), 0, TS), jax.random.fold_in(key_of[6], 1), 0, TS - 1).astype(jnp.int32)
    channel_freq = jnp.clip(0.856 + 0.856 * jax.random.uniform(key_of[7], (CHANNELS,), jnp.float32) ** steps_of(key_of[7], (CHANNELS,), ((0, 4),), -0.2, 0.2), 0.856, 1.712)
    return {"vis_values": vis_values, "kernel_u": kernel_u, "kernel_v": kernel_v, "offset_u": offset_u, "offset_v": offset_v, "block_owner": block_owner, "tile_slot": tile_slot, "channel_freq": channel_freq}


def grid_channel(vis, kern_u, kern_v, offs_u, offs_v):
    row_grid = jnp.arange(TU, dtype=jnp.int32)[None, :, None]
    col_grid = jnp.arange(TV, dtype=jnp.int32)[None, None, :]
    spread_u = jnp.zeros((vis.shape[0], TU, BV), jnp.float32)
    spread_v = jnp.zeros((vis.shape[0], BV, TV), jnp.float32)
    for tap_index in range(TAPS):
        spread_u = spread_u + jnp.where(row_grid == offs_u[:, None, :] + tap_index, kern_u[:, tap_index:tap_index + 1, :].astype(jnp.float32), 0.0)
        spread_v = spread_v + jnp.where(col_grid == offs_v[:, :, None] + tap_index, kern_v[:, tap_index, :, None].astype(jnp.float32), 0.0)
    left = (vis.astype(jnp.float32)[:, :, None, :] * spread_u[:, None, :, :]).astype(jnp.bfloat16)
    left = lax.optimization_barrier(left)
    return jnp.einsum('bpin,bnj->bpij', left.astype(jnp.float32), spread_v)

def reference(vis_values, kernel_u, kernel_v, offset_u, offset_v, block_owner, tile_slot, channel_freq):
    tiles_slab = GRID // N_ROW // TU * (GRID // TV)
    image_scale = 1.0 / math.sqrt(BLOCKS * BV)

    def one_channel(total, inputs):
        vis, kern_u, kern_v, offs_u, offs_v, owner_row, slot_row, frequency = inputs
        contribution = grid_channel(vis, kern_u, kern_v, offs_u, offs_v)
        tile_ids = (owner_row[:, 0] * tiles_slab + slot_row).astype(jnp.int32)
        tiles_all = jnp.zeros((N_ROW * tiles_slab, 2, TU, TV), jnp.float32).at[tile_ids].add(contribution)
        uv_grid = tiles_all.reshape(GRID // TU, GRID // TV, 2, TU, TV).transpose(2, 0, 3, 1, 4).reshape(2, GRID, GRID)
        field = lax.complex(uv_grid[0], uv_grid[1])
        dirty_image = jnp.real(jnp.fft.ifft2(field)) * (GRID * GRID * image_scale)
        offset_freq = (frequency - 1.284) / 0.428
        weights = jnp.stack([jnp.ones_like(offset_freq), offset_freq, offset_freq * offset_freq])
        taylor_terms = (weights[:, None, None] * dirty_image[None]).astype(jnp.bfloat16)
        return (total + taylor_terms.astype(jnp.float32), None)
    start = jnp.zeros((3, GRID, GRID), jnp.float32)
    total, _ = lax.scan(one_channel, start, (vis_values, kernel_u, kernel_v, offset_u, offset_v, block_owner, tile_slot, channel_freq))
    return total.astype(jnp.bfloat16)
```

```python
import math

import jax
import jax.numpy as jnp
import ml_dtypes
import numpy as np
from jax import lax
from jax.experimental import pallas as pl
from jax.experimental.pallas import tpu as pltpu
from jax.sharding import PartitionSpec as P

GRID = 4096
TU = 16
TV = 128
BANDS = GRID // TU
TILE_COLS = GRID // TV
BF16 = ml_dtypes.bfloat16
VMEM_LIMIT = 56 * 1024 * 1024


def turn(index, length):
    angle = 2.0 * np.pi * (index % length) / length
    return np.cos(angle), np.sin(angle)


def tile_tables(row_count):
    width = GRID // row_count
    j = np.arange(TV)[:, None]
    m = np.arange(GRID)[None, :]
    cos, sin = turn(j * m, GRID)
    cos = cos.reshape(TV, row_count, width).transpose(1, 0, 2)
    sin = sin.reshape(TV, row_count, width).transpose(1, 0, 2)
    top = np.concatenate([cos, sin], axis=2)
    low = np.concatenate([-sin, cos], axis=2)
    return np.concatenate([top, low], axis=1).astype(BF16)


def phase_table(width):
    cos, sin = turn(np.arange(TILE_COLS)[:, None] * np.arange(width)[None, :], TILE_COLS)
    return np.stack([cos, sin], axis=1).reshape(2 * TILE_COLS, width).astype(np.float32)


def band_table(scale):
    index = np.arange(BANDS)
    cos, sin = turn(index[:, None] * index[None, :], BANDS)
    return (np.block([[cos, -sin], [sin, cos]]) * scale).astype(BF16)


def inner_table():
    groups = BANDS // 16
    g = np.arange(groups)[:, None, None, None]
    high = np.arange(TU)[None, :, None, None]
    low = np.arange(16)[None, None, :, None]
    i = np.arange(TU)[None, None, None, :]
    cos, sin = turn(i * (16 * g + low + BANDS * high), GRID)
    parts = np.stack([cos, -sin], axis=4)
    full = parts[..., None] * np.eye(16)[None, None, :, None, None, :]
    return full.reshape(groups, TU * 16, TU * 2 * 16).astype(BF16)


def grid_kernel(vis_ref, ku_ref, kv_ref, ou_ref, ov_ref, ids_ref, out_ref):
    blocks, taps = ku_ref.shape[0], ku_ref.shape[1]

    def one(b, carry):
        d_u = lax.broadcasted_iota(jnp.int32, (TU, TV), 0) - ou_ref[pl.ds(b, 1), :]
        d_v = lax.broadcasted_iota(jnp.int32, (TV, TV), 0) - ov_ref[pl.ds(b, 1), :]
        ku = ku_ref[b].astype(jnp.float32)
        kv = kv_ref[b].astype(jnp.float32)
        vis = vis_ref[b].astype(jnp.float32)
        spread_u = jnp.zeros((TU, TV), jnp.float32)
        spread_v = jnp.zeros((TV, TV), jnp.float32)
        for t in range(taps):
            spread_u = jnp.where(d_u == t, ku[t : t + 1], spread_u)
            spread_v = jnp.where(d_v == t, kv[t : t + 1], spread_v)
        left = jnp.concatenate([vis[0:1] * spread_u, vis[1:2] * spread_u], axis=0)
        tile = lax.dot_general(
            left.astype(jnp.bfloat16),
            spread_v.astype(jnp.bfloat16),
            (((1,), (1,)), ((), ())),
            preferred_element_type=jnp.float32,
        ).astype(jnp.bfloat16)
        out_ref[b] = jnp.concatenate([tile[:TU], tile[TU:]], axis=1)
        return carry

    lax.fori_loop(0, blocks, one, 0, unroll=4)
    out_ref[blocks] = ids_ref[...]


def column_kernel(meta_ref, band_ref, col_ref, tile_ref, table_ref, phase_ref, out_ref, acc_ref):
    step = pl.program_id(0)
    blocks = tile_ref.shape[1] - 1
    width = phase_ref.shape[1]
    chunk = 16

    @pl.when(step == 0)
    def _():
        acc_ref[...] = jnp.zeros_like(acc_ref)

    def some(q, carry):
        tiles = tile_ref[0, pl.ds(q * chunk, chunk)].reshape(chunk * TU, 2 * TV)
        cols = jnp.dot(tiles, table_ref[0], preferred_element_type=jnp.float32)
        for k in range(chunk):
            at = step * blocks + q * chunk + k
            band = band_ref[at]
            col = col_ref[at]
            cos = phase_ref[pl.ds(2 * col, 1), :]
            sin = phase_ref[pl.ds(2 * col + 1, 1), :]
            real = cols[k * TU : (k + 1) * TU, :width]
            imag = cols[k * TU : (k + 1) * TU, width:]
            rows = pl.ds(pl.multiple_of(band * TU, TU), TU)
            sum_real = real * cos - imag * sin
            sum_imag = real * sin + imag * cos
            for s in range(width // 128):
                acc_ref[s, rows, :] += sum_real[:, s * 128 : (s + 1) * 128]
                acc_ref[width // 128 + s, rows, :] += sum_imag[:, s * 128 : (s + 1) * 128]
        return carry

    lax.fori_loop(0, blocks // chunk, some, 0)

    @pl.when(step == pl.num_programs(0) - 1)
    def _():
        for i in range(TU):
            for s in range(2 * width // 128):
                part, at = divmod(s * 128, width)
                rows = acc_ref[s, pl.ds(i, BANDS, stride=TU), :]
                out_ref[i, pl.ds(part * BANDS, BANDS), pl.ds(at, 128)] = rows.astype(jnp.bfloat16)


def row_kernel(x_ref, band_ref, inner_ref, out_ref, mid_ref):
    width = x_ref.shape[2]

    def first(i, carry):
        y = jnp.dot(band_ref[...], x_ref[i], preferred_element_type=jnp.float32)
        mid_ref[pl.ds(2 * i, 2)] = y.astype(jnp.bfloat16).reshape(2, BANDS, width)
        return carry

    lax.fori_loop(0, TU, first, 0)

    def second(g, carry):
        rows = pl.ds(pl.multiple_of(g * 16, 16), 16)
        y = mid_ref[:, rows, :].reshape(2 * TU * 16, width)
        z = jnp.dot(inner_ref[g], y, preferred_element_type=jnp.float32)
        out_ref[:, rows, :] = z.astype(jnp.bfloat16).reshape(TU, 16, width)
        return carry

    lax.fori_loop(0, BANDS // 16, second, 0)


def shards(
    vis_values, kernel_u, kernel_v, offset_u, offset_v, block_owner, tile_slot, channel_freq
):
    row_count = lax.axis_size("row")
    freq_count = lax.axis_size("freq")
    blocks = vis_values.shape[1]
    vis_count = vis_values.shape[3]
    width = GRID // row_count
    tiles_slab = GRID // row_count // TU * TILE_COLS
    vmem = pl.BlockSpec(memory_space=pltpu.VMEM)
    params = pltpu.CompilerParams(vmem_limit_bytes=VMEM_LIMIT)

    freqs = lax.all_gather(channel_freq[0], "freq")
    tile = block_owner[0, :, 0] * tiles_slab + tile_slot[0]
    ids = jnp.stack([tile // TILE_COLS, tile % TILE_COLS]).astype(jnp.bfloat16)
    ids = jnp.pad(ids, ((0, TU - 2), (0, 2 * TV - blocks)))
    with jax.named_scope("gridding"):
        tiles = pl.pallas_call(
            grid_kernel,
            out_shape=jax.ShapeDtypeStruct((blocks + 1, TU, 2 * TV), jnp.bfloat16),
            in_specs=[vmem] * 6,
            out_specs=vmem,
            compiler_params=params,
        )(vis_values[0], kernel_u[0], kernel_v[0], offset_u[0], offset_v[0], ids)
    tiles = lax.all_gather(tiles, "row")
    ids = tiles[:, blocks, :2, :blocks].astype(jnp.int32)
    meta = lax.axis_index("row").astype(jnp.int32).reshape(1)
    with jax.named_scope("columns"):
        spectrum = pl.pallas_call(
            column_kernel,
            out_shape=jax.ShapeDtypeStruct((TU, 2 * BANDS, width), jnp.bfloat16),
            grid_spec=pltpu.PrefetchScalarGridSpec(
                num_scalar_prefetch=3,
                grid=(row_count,),
                in_specs=[
                    pl.BlockSpec((1, blocks + 1, TU, 2 * TV), lambda g, *_: (g, 0, 0, 0)),
                    pl.BlockSpec((1, 2 * TV, 2 * width), lambda g, meta, *_: (meta[0], 0, 0)),
                    pl.BlockSpec((2 * TILE_COLS, width), lambda g, *_: (0, 0)),
                ],
                out_specs=pl.BlockSpec((TU, 2 * BANDS, width), lambda g, *_: (0, 0, 0)),
                scratch_shapes=[pltpu.VMEM((2 * width // 128, GRID, 128), jnp.float32)],
            ),
            compiler_params=params,
        )(
            meta,
            ids[:, 0].reshape(-1),
            ids[:, 1].reshape(-1),
            tiles,
            tile_tables(row_count),
            phase_table(width),
        )
    scale = 1.0 / math.sqrt(blocks * row_count * vis_count)
    with jax.named_scope("rows"):
        dirty = pl.pallas_call(
            row_kernel,
            out_shape=jax.ShapeDtypeStruct((TU, BANDS, width), jnp.bfloat16),
            in_specs=[vmem] * 3,
            out_specs=vmem,
            scratch_shapes=[pltpu.VMEM((2 * TU, BANDS, width), jnp.bfloat16)],
            compiler_params=params,
        )(spectrum, band_table(scale), inner_table())
    dirty = dirty.reshape(freq_count, GRID // freq_count, width)
    dirty = lax.all_to_all(dirty, "freq", split_axis=0, concat_axis=0, tiled=True)
    x = (freqs - 1.284) / 0.428
    weights = jnp.stack([jnp.ones_like(x), x, x * x])
    outs = []
    for k in range(3):
        total = jnp.zeros(dirty.shape[1:], jnp.float32)
        for c in range(freq_count):
            total = total + (weights[k, c] * dirty[c].astype(jnp.float32))
        outs.append(total.astype(jnp.bfloat16))
    return jnp.stack(outs)


def solution(mesh):
    return jax.shard_map(
        shards,
        mesh=mesh,
        in_specs=(
            P("freq", "row", None, None),
            P("freq", "row", None, None),
            P("freq", "row", None, None),
            P("freq", "row", None),
            P("freq", "row", None),
            P("freq", "row", None),
            P("freq", "row"),
            P("freq"),
        ),
        out_specs=P(None, "freq", "row"),
        check_vma=False,
    )
```

```python
from functools import partial
import math

import jax
import jax.numpy as jnp
import ml_dtypes
import numpy as np
from jax import lax
from jax.experimental import pallas as pl
from jax.experimental.pallas import tpu as pltpu
from jax.sharding import PartitionSpec as P

GRID = 4096
TU = 16
TV = 128
BANDS = GRID // TU
TILE_COLS = GRID // TV
BF16 = ml_dtypes.bfloat16
VMEM_LIMIT = 56 * 1024 * 1024


def turn(index, length):
    angle = 2.0 * np.pi * (index % length) / length
    return np.cos(angle), np.sin(angle)


def tile_tables(row_count, chunk):
    j = np.arange(TV)[:, None]
    m = np.arange(GRID)[None, :]
    cos, sin = turn(j * m, GRID)
    cos = cos.reshape(TV, row_count, -1, chunk).transpose(1, 2, 0, 3)
    sin = sin.reshape(TV, row_count, -1, chunk).transpose(1, 2, 0, 3)
    top = np.concatenate([cos, sin], axis=3)
    low = np.concatenate([-sin, cos], axis=3)
    return np.concatenate([top, low], axis=2).astype(BF16)


def phase_table(chunk):
    cos, sin = turn(np.arange(TILE_COLS)[:, None] * np.arange(chunk)[None, :], TILE_COLS)
    whole = np.concatenate([cos, sin], axis=1).astype(np.float32)
    main = whole.astype(BF16)
    return np.concatenate([main, (whole - main.astype(np.float32)).astype(BF16)], axis=0)


def band_table(scale):
    index = np.arange(BANDS)
    cos, sin = turn(index[:, None] * index[None, :], BANDS)
    return (np.concatenate([cos, sin], axis=0) * scale).astype(BF16)


def inner_table():
    groups = BANDS // 16
    g = np.arange(groups)[:, None, None, None]
    high = np.arange(TU)[None, :, None, None]
    low = np.arange(16)[None, None, :, None]
    i = np.arange(TU)[None, None, None, :]
    cos, sin = turn(i * (16 * g + low + BANDS * high), GRID)
    parts = np.stack([cos, -sin], axis=4)
    full = parts[..., None] * np.eye(16)[None, None, :, None, None, :]
    return full.reshape(groups, TU * 16, TU * 2 * 16).astype(BF16)


def grid_kernel(vis_ref, ku_ref, kv_ref, ou_ref, ov_ref, ids_ref, out_ref, tile_ref):
    blocks, taps = ku_ref.shape[0], ku_ref.shape[1]

    def one(b, carry):
        d_u = lax.broadcasted_iota(jnp.int32, (TU, TV), 0) - ou_ref[pl.ds(b, 1), :]
        d_v = lax.broadcasted_iota(jnp.int32, (TV, TV), 0) - ov_ref[pl.ds(b, 1), :]
        ku = ku_ref[b].astype(jnp.float32)
        kv = kv_ref[b].astype(jnp.float32)
        vis = vis_ref[b].astype(jnp.float32)
        spread_u = jnp.zeros((TU, TV), jnp.float32)
        spread_v = jnp.zeros((TV, TV), jnp.float32)
        for t in range(taps):
            spread_u = jnp.where(d_u == t, ku[t : t + 1], spread_u)
            spread_v = jnp.where(d_v == t, kv[t : t + 1], spread_v)
        left = jnp.concatenate([vis[0:1] * spread_u, vis[1:2] * spread_u], axis=0)
        tile = lax.dot_general(
            left.astype(jnp.bfloat16),
            spread_v.astype(jnp.bfloat16),
            (((1,), (1,)), ((), ())),
            preferred_element_type=jnp.float32,
        )
        for i in range(TU):
            tile_ref[i, pl.ds(b, 1), :] = tile[i : i + 1]
            tile_ref[TU + i, pl.ds(b, 1), :] = tile[TU + i : TU + i + 1]
        return carry

    lax.fori_loop(0, blocks, one, 0, unroll=4)
    out_ref[:TU, :, :TV] = tile_ref[:TU].astype(jnp.bfloat16)
    out_ref[:TU, :, TV:] = tile_ref[TU:].astype(jnp.bfloat16)
    out_ref[TU] = ids_ref[...]


def image_kernel(
    freq_count,
    tiles_ref,
    band_ref,
    col_ref,
    x_ref,
    tile_table_ref,
    phase_table_ref,
    band_table_ref,
    inner_ref,
    out_ref,
    factor_ref,
    phase_ref,
    mid_ref,
    send_ref,
    recv_ref,
    x_recv_ref,
    send_sem,
    recv_sem,
    x_send_sem,
    x_recv_sem,
):
    me = lax.axis_index("freq")
    blocks = tiles_ref.shape[0] * tiles_ref.shape[2]
    chunks, chunk = send_ref.shape[0], send_ref.shape[3]
    share = TU // freq_count
    half = freq_count // 2
    shifts = sorted(range(1, freq_count), key=lambda d: abs(d - half))
    peers = [lax.rem(me + d, freq_count) for d in shifts]

    barrier = pltpu.get_barrier_semaphore()
    for peer in peers:
        pl.semaphore_signal(
            barrier, inc=1, device_id={"freq": peer}, device_id_type=pl.DeviceIdType.MESH
        )

    bands = lax.broadcasted_iota(jnp.int32, (BANDS, blocks), 0) == band_ref[...]
    picked = jnp.dot(
        band_table_ref[...],
        bands.astype(jnp.float32).astype(jnp.bfloat16),
        preferred_element_type=jnp.float32,
    ).astype(jnp.bfloat16)
    factor_ref[:BANDS, :blocks] = picked[:BANDS]
    factor_ref[:BANDS, blocks:] = -picked[BANDS:]
    factor_ref[BANDS:, :blocks] = picked[BANDS:]
    factor_ref[BANDS:, blocks:] = picked[:BANDS]
    at = lax.broadcasted_iota(jnp.int32, (2 * TILE_COLS, blocks), 0)
    cols = (at == col_ref[...]) | (at == col_ref[...] + TILE_COLS)
    phase_ref[...] = lax.dot_general(
        cols.astype(jnp.float32).astype(jnp.bfloat16),
        phase_table_ref[...],
        (((0,), (0,)), ((), ())),
        preferred_element_type=jnp.float32,
    )

    copies = []
    for q in range(chunks):

        def first(i, carry):
            tiles = tiles_ref[:, pl.ds(i, 1)].reshape(blocks, 2 * TV)
            cols = jnp.dot(tiles, tile_table_ref[q], preferred_element_type=jnp.float32)
            real, imag = cols[:, :chunk], cols[:, chunk:]
            cos, sin = phase_ref[:, :chunk], phase_ref[:, chunk:]
            turned = jnp.concatenate(
                [
                    (real * cos - imag * sin).astype(jnp.bfloat16),
                    (real * sin + imag * cos).astype(jnp.bfloat16),
                ],
                axis=0,
            )
            y = jnp.dot(factor_ref[...], turned, preferred_element_type=jnp.float32)
            mid_ref[pl.ds(2 * i, 2)] = y.astype(jnp.bfloat16).reshape(2, BANDS, chunk)
            return carry

        lax.fori_loop(0, TU, first, 0)

        def second(g, carry):
            rows = pl.ds(pl.multiple_of(g * 16, 16), 16)
            y = mid_ref[:, rows, :].reshape(2 * TU * 16, chunk)
            z = jnp.dot(inner_ref[g], y, preferred_element_type=jnp.float32)
            send_ref[q, :, rows, :] = z.astype(jnp.bfloat16).reshape(TU, 16, chunk)
            return carry

        lax.fori_loop(0, BANDS // 16, second, 0)

        if q == 0:
            pl.semaphore_wait(barrier, freq_count - 1)
            for s, peer in enumerate(peers):
                copy = pltpu.make_async_remote_copy(
                    src_ref=x_ref,
                    dst_ref=x_recv_ref.at[s],
                    send_sem=x_send_sem.at[s],
                    recv_sem=x_recv_sem.at[s],
                    device_id={"freq": peer},
                    device_id_type=pl.DeviceIdType.MESH,
                )
                copy.start()
                copies.append(copy)
        for s, peer in enumerate(peers):
            copy = pltpu.make_async_remote_copy(
                src_ref=send_ref.at[q, pl.ds(peer * share, share)],
                dst_ref=recv_ref.at[q, s],
                send_sem=send_sem.at[q, s],
                recv_sem=recv_sem.at[q, s],
                device_id={"freq": peer},
                device_id_type=pl.DeviceIdType.MESH,
            )
            copy.start()
            copies.append(copy)

    own = x_ref[0:1, :]
    for copy in copies[: freq_count - 1]:
        copy.wait()
    others = [x_recv_ref[s, 0:1, :] for s in range(freq_count - 1)]
    step = 32
    for q in range(chunks):
        for s in range(freq_count - 1):
            copies[(q + 1) * (freq_count - 1) + s].wait()

        def combine(at, carry):
            h = at // (BANDS // step)
            rows = pl.ds(pl.multiple_of(at % (BANDS // step) * step, step), step)
            image = send_ref[q, me * share + h, rows, :].astype(jnp.float32)
            total = [image, own * image, (own * own) * image]
            for s in range(freq_count - 1):
                image = recv_ref[q, s, h, rows, :].astype(jnp.float32)
                x = others[s]
                total[0] += image
                total[1] += x * image
                total[2] += (x * x) * image
            for k in range(3):
                out_ref[k, h, rows, q * chunk : (q + 1) * chunk] = total[k].astype(jnp.bfloat16)
            return carry

        lax.fori_loop(0, share * (BANDS // step), combine, 0)


def shards(
    vis_values, kernel_u, kernel_v, offset_u, offset_v, block_owner, tile_slot, channel_freq
):
    row_count = lax.axis_size("row")
    freq_count = lax.axis_size("freq")
    blocks = vis_values.shape[1]
    vis_count = vis_values.shape[3]
    width = GRID // row_count
    tiles_slab = GRID // row_count // TU * TILE_COLS
    vmem = pl.BlockSpec(memory_space=pltpu.VMEM)
    params = pltpu.CompilerParams(vmem_limit_bytes=VMEM_LIMIT)

    chunk = min(256, width)
    chunks = width // chunk
    peers = freq_count - 1
    share = TU // freq_count

    tile = block_owner[0, :, 0] * tiles_slab + tile_slot[0]
    ids = jnp.stack([tile // TILE_COLS, tile % TILE_COLS]).astype(jnp.bfloat16)
    ids = jnp.pad(ids, ((0, blocks - 2), (0, 2 * TV - blocks)))
    with jax.named_scope("gridding"):
        tiles = pl.pallas_call(
            grid_kernel,
            out_shape=jax.ShapeDtypeStruct((TU + 1, blocks, 2 * TV), jnp.bfloat16),
            in_specs=[vmem] * 6,
            out_specs=vmem,
            scratch_shapes=[pltpu.VMEM((2 * TU, blocks, TV), jnp.float32)],
            compiler_params=params,
        )(vis_values[0], kernel_u[0], kernel_v[0], offset_u[0], offset_v[0], ids)
    tiles = lax.all_gather(tiles, "row")
    ids = tiles[:, TU, :2, :blocks].astype(jnp.int32)
    x = jnp.broadcast_to((channel_freq - 1.284) / 0.428, (8, chunk))
    table = lax.dynamic_index_in_dim(
        jnp.asarray(tile_tables(row_count, chunk)), lax.axis_index("row"), 0, keepdims=False
    )
    scale = 1.0 / math.sqrt(blocks * row_count * vis_count)
    total_blocks = row_count * blocks
    with jax.named_scope("image"):
        image = pl.pallas_call(
            partial(image_kernel, freq_count),
            out_shape=jax.ShapeDtypeStruct((3, share, BANDS, width), jnp.bfloat16),
            in_specs=[vmem] * 8,
            out_specs=vmem,
            scratch_shapes=[
                pltpu.VMEM((2 * BANDS, 2 * total_blocks), jnp.bfloat16),
                pltpu.VMEM((total_blocks, 2 * chunk), jnp.float32),
                pltpu.VMEM((2 * TU, BANDS, chunk), jnp.bfloat16),
                pltpu.VMEM((chunks, TU, BANDS, chunk), jnp.bfloat16),
                pltpu.VMEM((chunks, peers, share, BANDS, chunk), jnp.bfloat16),
                pltpu.VMEM((peers, 8, chunk), jnp.float32),
                pltpu.SemaphoreType.DMA((chunks, peers)),
                pltpu.SemaphoreType.DMA((chunks, peers)),
                pltpu.SemaphoreType.DMA((peers,)),
                pltpu.SemaphoreType.DMA((peers,)),
            ],
            compiler_params=pltpu.CompilerParams(
                vmem_limit_bytes=VMEM_LIMIT, collective_id=0, has_side_effects=True
            ),
        )(
            tiles,
            ids[:, 0].reshape(1, -1),
            ids[:, 1].reshape(1, -1),
            x,
            table,
            phase_table(chunk),
            band_table(scale),
            inner_table(),
        )
    return image.reshape(3, GRID // freq_count, width)


def solution(mesh):
    return jax.shard_map(
        shards,
        mesh=mesh,
        in_specs=(
            P("freq", "row", None, None),
            P("freq", "row", None, None),
            P("freq", "row", None, None),
            P("freq", "row", None),
            P("freq", "row", None),
            P("freq", "row", None),
            P("freq", "row"),
            P("freq"),
        ),
        out_specs=P(None, "freq", "row"),
        check_vma=False,
    )
```

```python
from functools import partial
import math

import jax
import jax.numpy as jnp
import ml_dtypes
import numpy as np
from jax import lax
from jax.experimental import pallas as pl
from jax.experimental.pallas import tpu as pltpu
from jax.sharding import PartitionSpec as P

GRID = 4096
TU = 16
TV = 128
BANDS = GRID // TU
TILE_COLS = GRID // TV
BF16 = ml_dtypes.bfloat16
VMEM_LIMIT = 56 * 1024 * 1024


def turn(index, length):
    angle = 2.0 * np.pi * (index % length) / length
    return np.cos(angle), np.sin(angle)


def tile_tables(row_count, chunk):
    j = np.arange(TV)[:, None]
    m = np.arange(GRID)[None, :]
    cos, sin = turn(j * m, GRID)
    cos = cos.reshape(TV, row_count, -1, chunk).transpose(1, 2, 0, 3)
    sin = sin.reshape(TV, row_count, -1, chunk).transpose(1, 2, 0, 3)
    top = np.concatenate([cos, sin], axis=3)
    low = np.concatenate([-sin, cos], axis=3)
    return np.concatenate([top, low], axis=2).astype(BF16)


def phase_table(chunk):
    cos, sin = turn(np.arange(TILE_COLS)[:, None] * np.arange(chunk)[None, :], TILE_COLS)
    whole = np.concatenate([cos, sin], axis=1).astype(np.float32)
    main = whole.astype(BF16)
    return np.concatenate([main, (whole - main.astype(np.float32)).astype(BF16)], axis=0)


def band_table(scale):
    index = np.arange(BANDS)
    cos, sin = turn(index[:, None] * index[None, :], BANDS)
    return (np.concatenate([cos, sin], axis=0) * scale).astype(BF16)


def inner_table():
    groups = BANDS // 16
    g = np.arange(groups)[:, None, None, None]
    high = np.arange(TU)[None, :, None, None]
    low = np.arange(16)[None, None, :, None]
    i = np.arange(TU)[None, None, None, :]
    cos, sin = turn(i * (16 * g + low + BANDS * high), GRID)
    parts = np.stack([cos, -sin], axis=4)
    full = parts[..., None] * np.eye(16)[None, None, :, None, None, :]
    return full.reshape(groups, TU * 16, TU * 2 * 16).astype(BF16)


def grid_tiles(vis_ref, ku_ref, kv_ref, ou_ref, ov_ref, tile_ref):
    blocks, taps = ku_ref.shape[1], ku_ref.shape[2]

    def one(b, carry):
        d_u = lax.broadcasted_iota(jnp.int32, (TU, TV), 0) - ou_ref[0, pl.ds(b, 1), :]
        d_v = lax.broadcasted_iota(jnp.int32, (TV, TV), 0) - ov_ref[0, pl.ds(b, 1), :]
        ku = ku_ref[0, b].astype(jnp.float32)
        kv = kv_ref[0, b].astype(jnp.float32)
        vis = vis_ref[0, b].astype(jnp.float32)
        spread_u = jnp.zeros((TU, TV), jnp.float32)
        spread_v = jnp.zeros((TV, TV), jnp.float32)
        for t in range(taps):
            spread_u = jnp.where(d_u == t, ku[t : t + 1], spread_u)
            spread_v = jnp.where(d_v == t, kv[t : t + 1], spread_v)
        left = jnp.concatenate([vis[0:1] * spread_u, vis[1:2] * spread_u], axis=0)
        tile = lax.dot_general(
            left.astype(jnp.bfloat16),
            spread_v.astype(jnp.bfloat16),
            (((1,), (1,)), ((), ())),
            preferred_element_type=jnp.float32,
        )
        for i in range(TU):
            tile_ref[i, pl.ds(b, 1), :] = tile[i : i + 1]
            tile_ref[TU + i, pl.ds(b, 1), :] = tile[TU + i : TU + i + 1]
        return carry

    lax.fori_loop(0, blocks, one, 0, unroll=4)


def image_kernel(
    freq_count,
    row_count,
    vis_ref,
    ku_ref,
    kv_ref,
    ou_ref,
    ov_ref,
    ids_ref,
    x_ref,
    phase_table_ref,
    band_table_ref,
    tile_table_hbm,
    inner_hbm,
    out_ref,
    grid_ref,
    tiles_ref,
    tile_table_ref,
    inner_ref,
    factor_ref,
    phase_ref,
    mid_ref,
    send_ref,
    recv_ref,
    x_send_ref,
    x_recv_ref,
    table_sem,
    swap_sem,
    row_send,
    row_recv,
    core_send,
    core_recv,
    send_sem,
    recv_sem,
    x_send_sem,
    x_recv_sem,
):
    me, row = lax.axis_index("freq"), lax.axis_index("row")
    block_count = ku_ref.shape[1]
    blocks = row_count * block_count
    chunks, chunk = send_ref.shape[1], send_ref.shape[4]
    share = TU // freq_count
    half = freq_count // 2
    first_of_half = me // half * half
    partner = lax.rem(me + half, freq_count)
    group = [first_of_half + lax.rem(me - first_of_half + d, half) for d in range(1, half)]
    pairs = row_count // 2
    pair, sub = row // 2, lax.rem(row, 2)
    sibling = pair * 2 + 1 - sub
    targets = [lax.rem(pair + d, pairs) * 2 + sub for d in range(1, pairs)]
    sources = [lax.rem(pair + pairs - d, pairs) * 2 + sub for d in range(1, pairs)]
    everyone = [{"freq": f} for f in [partner] + group] + [{"row": r} for r in [sibling] + targets]

    barrier = pltpu.get_barrier_semaphore()
    for device in everyone:
        pl.semaphore_signal(
            barrier, inc=1, device_id=device, device_id_type=pl.DeviceIdType.MESH
        )
    inner_rows = pl.ds(first_of_half * share * 16, TU // 2 * 16)
    tables = [
        pltpu.make_async_copy(tile_table_hbm.at[row], tile_table_ref, table_sem.at[0]),
        pltpu.make_async_copy(inner_hbm.at[:, inner_rows, :], inner_ref, table_sem.at[1]),
    ]
    for copy in tables:
        copy.start()

    grid_tiles(vis_ref, ku_ref, kv_ref, ou_ref, ov_ref, grid_ref)
    for i in range(TU):
        rows = slice(i * block_count, (i + 1) * block_count)
        tiles_ref[0, row, rows, :TV] = grid_ref[i].astype(jnp.bfloat16)
        tiles_ref[0, row, rows, TV:] = grid_ref[TU + i].astype(jnp.bfloat16)
    meta_rows = slice(TU * block_count, TU * block_count + 16)
    x = x_ref[...]
    x_main = x.astype(jnp.bfloat16).astype(jnp.float32)
    x_next = (x - x_main).astype(jnp.bfloat16).astype(jnp.float32)
    x_last = x - x_main - x_next
    line = lax.broadcasted_iota(jnp.int32, (16, 2 * TV), 0)
    meta = jnp.where(line == 2, x_main, ids_ref[...])
    meta = jnp.where(line == 3, x_next, jnp.where(line == 4, x_last, meta))
    tiles_ref[0, row, meta_rows, :] = meta.astype(jnp.bfloat16)

    def remote(src, dst, send, recv, device):
        copy = pltpu.make_async_remote_copy(
            src_ref=src,
            dst_ref=dst,
            send_sem=send,
            recv_sem=recv,
            device_id=device,
            device_id_type=pl.DeviceIdType.MESH,
        )
        copy.start()
        return copy

    def to_rows(c):
        own = tiles_ref.at[c, row]
        direct = [
            remote(own, own, row_send.at[c, n], row_recv.at[c, n], {"row": target})
            for n, target in enumerate(targets)
        ]
        return direct, [
            remote(own, own, core_send.at[c, 0], core_recv.at[c, 0], {"row": sibling})
        ]

    def forward(c, direct):
        passed = []
        for n, source in enumerate(sources):
            direct[n].wait_recv()
            block = tiles_ref.at[c, source]
            passed.append(
                remote(
                    block,
                    block,
                    core_send.at[c, n + 1],
                    core_recv.at[c, n + 1],
                    {"row": sibling},
                )
            )
        return passed

    pl.semaphore_wait(barrier, len(everyone))
    swap = remote(
        tiles_ref.at[0, row],
        tiles_ref.at[1, row],
        swap_sem.at[0],
        swap_sem.at[1],
        {"freq": partner},
    )
    direct_a, near_a = to_rows(0)
    near_a += forward(0, direct_a)
    swap.wait_recv()
    direct_b, near_b = to_rows(1)

    def x_of(c):
        meta = tiles_ref[c, row, meta_rows, :].astype(jnp.float32)
        return meta[2:3] + (meta[3:4] + meta[4:5])

    x_own = [x_of(0)[:, :chunk], x_of(1)[:, :chunk]]
    for c in range(2):
        x_send_ref[c * 8 : (c + 1) * 8, :] = jnp.broadcast_to(x_own[c], (8, chunk))
    x_copies = [
        remote(x_send_ref, x_recv_ref.at[n], x_send_sem.at[n], x_recv_sem.at[n], {"freq": peer})
        for n, peer in enumerate(group)
    ]
    for copy in near_a:
        copy.wait_recv()
    for copy in tables:
        copy.wait()

    def channel(c):
        for p in range(pairs):
            at = meta_rows.start
            ids = (
                tiles_ref[c, 2 * p, at : at + 16, :TV].astype(jnp.float32)
                + tiles_ref[c, 2 * p + 1, at : at + 16, :TV].astype(jnp.float32)
            )
            ids = ids.astype(jnp.int32)
            lanes = slice(p * TV, (p + 1) * TV)
            bands = lax.broadcasted_iota(jnp.int32, (BANDS, TV), 0) == ids[0:1]
            picked = jnp.dot(
                band_table_ref[...],
                bands.astype(jnp.float32).astype(jnp.bfloat16),
                preferred_element_type=jnp.float32,
            ).astype(jnp.bfloat16)
            imag_lanes = slice(blocks + p * TV, blocks + (p + 1) * TV)
            factor_ref[:BANDS, lanes] = picked[:BANDS]
            factor_ref[:BANDS, imag_lanes] = -picked[BANDS:]
            factor_ref[BANDS:, lanes] = picked[BANDS:]
            factor_ref[BANDS:, imag_lanes] = picked[:BANDS]
            at = lax.broadcasted_iota(jnp.int32, (2 * TILE_COLS, TV), 0)
            cols = (at == ids[1:2]) | (at == ids[1:2] + TILE_COLS)
            phase_ref[lanes, :] = lax.dot_general(
                cols.astype(jnp.float32).astype(jnp.bfloat16),
                phase_table_ref[...],
                (((0,), (0,)), ((), ())),
                preferred_element_type=jnp.float32,
            )

        copies = []
        for q in range(chunks):

            def first(i, carry):
                rows = pl.ds(pl.multiple_of(i * block_count, block_count), block_count)
                tiles = tiles_ref[c, :, rows, :].reshape(blocks, 2 * TV)
                cols = jnp.dot(tiles, tile_table_ref[q], preferred_element_type=jnp.float32)
                real, imag = cols[:, :chunk], cols[:, chunk:]
                cos, sin = phase_ref[:, :chunk], phase_ref[:, chunk:]
                turned = jnp.concatenate(
                    [
                        (real * cos - imag * sin).astype(jnp.bfloat16),
                        (real * sin + imag * cos).astype(jnp.bfloat16),
                    ],
                    axis=0,
                )
                y = jnp.dot(factor_ref[...], turned, preferred_element_type=jnp.float32)
                mid_ref[pl.ds(2 * i, 2)] = y.astype(jnp.bfloat16).reshape(2, BANDS, chunk)
                return carry

            lax.fori_loop(0, TU, first, 0)

            def second(g, carry):
                rows = pl.ds(pl.multiple_of(g * 16, 16), 16)
                y = mid_ref[:, rows, :].reshape(2 * TU * 16, chunk)
                z = jnp.dot(inner_ref[g], y, preferred_element_type=jnp.float32)
                send_ref[c, q, :, rows, :] = z.astype(jnp.bfloat16).reshape(TU // 2, 16, chunk)
                return carry

            lax.fori_loop(0, BANDS // 16, second, 0)
            for n, peer in enumerate(group):
                copies.append(
                    remote(
                        send_ref.at[c, q, pl.ds((peer - first_of_half) * share, share)],
                        recv_ref.at[c, q, n],
                        send_sem.at[c, q, n],
                        recv_sem.at[c, q, n],
                        {"freq": peer},
                    )
                )
        return copies

    images = channel(0)
    near_b += forward(1, direct_b)
    for copy in near_b:
        copy.wait_recv()
    images += channel(1)

    for copy in x_copies:
        copy.wait()
    for copy in direct_a + direct_b + near_a + near_b + [swap]:
        copy.wait_send()
    step = 32
    for q in range(chunks):
        for c in range(2):
            for n in range(half - 1):
                images[(c * chunks + q) * (half - 1) + n].wait()

        def combine(at, carry):
            h = at // (BANDS // step)
            rows = pl.ds(pl.multiple_of(at % (BANDS // step) * step, step), step)
            total = [jnp.zeros((step, chunk), jnp.float32) for _ in range(3)]
            for c in range(2):
                own_at = (me - first_of_half) * share + h
                terms = [(x_own[c], send_ref[c, q, own_at, rows, :])]
                for n in range(half - 1):
                    x_other = x_recv_ref[n, c * 8 : c * 8 + 1, :]
                    terms.append((x_other, recv_ref[c, q, n, h, rows, :]))
                for x_term, image in terms:
                    image = image.astype(jnp.float32)
                    total[0] += image
                    total[1] += x_term * image
                    total[2] += (x_term * x_term) * image
            for k in range(3):
                out_ref[k, h, rows, q * chunk : (q + 1) * chunk] = total[k].astype(jnp.bfloat16)
            return carry

        lax.fori_loop(0, share * (BANDS // step), combine, 0)


def shards(
    vis_values, kernel_u, kernel_v, offset_u, offset_v, block_owner, tile_slot, channel_freq
):
    row_count = lax.axis_size("row")
    freq_count = lax.axis_size("freq")
    blocks = vis_values.shape[1]
    vis_count = vis_values.shape[3]
    width = GRID // row_count
    tiles_slab = GRID // row_count // TU * TILE_COLS
    vmem = pl.BlockSpec(memory_space=pltpu.VMEM)
    chunk = min(256, width)
    chunks = width // chunk
    others = freq_count // 2 - 1
    share = TU // freq_count
    pairs = row_count // 2
    total_blocks = row_count * blocks

    tile = block_owner[0, :, 0] * tiles_slab + tile_slot[0]
    ids = jnp.stack([tile // TILE_COLS, tile % TILE_COLS]).astype(jnp.float32)
    odd = lax.axis_index("row") % 2
    ids = jnp.concatenate([jnp.where(odd == 0, ids, 0.0), jnp.where(odd == 1, ids, 0.0)], axis=1)
    ids = jnp.pad(ids, ((0, 14), (0, 2 * TV - 2 * blocks)))
    x = jnp.broadcast_to((channel_freq - 1.284) / 0.428, (16, 2 * TV))
    scale = 1.0 / math.sqrt(blocks * row_count * vis_count)
    dma = pltpu.SemaphoreType.DMA
    with jax.named_scope("image"):
        image = pl.pallas_call(
            partial(image_kernel, freq_count, row_count),
            out_shape=jax.ShapeDtypeStruct((3, share, BANDS, width), jnp.bfloat16),
            in_specs=[vmem] * 9 + [pl.BlockSpec(memory_space=pl.ANY)] * 2,
            out_specs=vmem,
            scratch_shapes=[
                pltpu.VMEM((2 * TU, blocks, TV), jnp.float32),
                pltpu.VMEM((2, row_count, TU * blocks + 16, 2 * TV), jnp.bfloat16),
                pltpu.VMEM((chunks, 2 * TV, 2 * chunk), jnp.bfloat16),
                pltpu.VMEM((BANDS // 16, TU // 2 * 16, 2 * TU * 16), jnp.bfloat16),
                pltpu.VMEM((2 * BANDS, 2 * total_blocks), jnp.bfloat16),
                pltpu.VMEM((total_blocks, 2 * chunk), jnp.float32),
                pltpu.VMEM((2 * TU, BANDS, chunk), jnp.bfloat16),
                pltpu.VMEM((2, chunks, TU // 2, BANDS, chunk), jnp.bfloat16),
                pltpu.VMEM((2, chunks, others, share, BANDS, chunk), jnp.bfloat16),
                pltpu.VMEM((16, chunk), jnp.float32),
                pltpu.VMEM((others, 16, chunk), jnp.float32),
                dma((2,)),
                dma((2,)),
                dma((2, pairs - 1)),
                dma((2, pairs - 1)),
                dma((2, pairs)),
                dma((2, pairs)),
                dma((2, chunks, others)),
                dma((2, chunks, others)),
                dma((others,)),
                dma((others,)),
            ],
            compiler_params=pltpu.CompilerParams(
                vmem_limit_bytes=VMEM_LIMIT, collective_id=0, has_side_effects=True
            ),
        )(
            vis_values,
            kernel_u,
            kernel_v,
            offset_u,
            offset_v,
            ids,
            x,
            phase_table(chunk),
            band_table(scale),
            tile_tables(row_count, chunk),
            inner_table(),
        )
    return image.reshape(3, GRID // freq_count, width)


def solution(mesh):
    return jax.shard_map(
        shards,
        mesh=mesh,
        in_specs=(
            P("freq", "row", None, None),
            P("freq", "row", None, None),
            P("freq", "row", None, None),
            P("freq", "row", None),
            P("freq", "row", None),
            P("freq", "row", None),
            P("freq", "row"),
            P("freq"),
        ),
        out_specs=P(None, "freq", "row"),
        check_vma=False,
    )
```

```python
from functools import partial
import math

import jax
import jax.numpy as jnp
import ml_dtypes
import numpy as np
from jax import lax
from jax.experimental import pallas as pl
from jax.experimental.pallas import tpu as pltpu
from jax.sharding import PartitionSpec as P

GRID = 4096
TU = 16
TV = 128
BANDS = GRID // TU
TILE_COLS = GRID // TV
BF16 = ml_dtypes.bfloat16
VMEM_LIMIT = 56 * 1024 * 1024


def turn(index, length):
    angle = 2.0 * np.pi * (index % length) / length
    return np.cos(angle), np.sin(angle)


def tile_tables(row_count, chunk):
    j = np.arange(TV)[:, None]
    m = np.arange(GRID)[None, :]
    cos, sin = turn(j * m, GRID)
    cos = cos.reshape(TV, row_count, -1, chunk).transpose(1, 2, 0, 3)
    sin = sin.reshape(TV, row_count, -1, chunk).transpose(1, 2, 0, 3)
    top = np.concatenate([cos, sin], axis=3)
    low = np.concatenate([-sin, cos], axis=3)
    return np.concatenate([top, low], axis=2).astype(BF16)


def phase_table(chunk):
    cos, sin = turn(np.arange(TILE_COLS)[:, None] * np.arange(chunk)[None, :], TILE_COLS)
    return np.concatenate([cos, sin], axis=1).astype(BF16)


def band_table(scale):
    index = np.arange(BANDS)
    cos, sin = turn(index[:, None] * index[None, :], BANDS)
    return (np.concatenate([cos, sin], axis=0) * scale).astype(BF16)


def inner_table():
    groups = BANDS // 16
    g = np.arange(groups)[:, None, None, None]
    high = np.arange(TU)[None, :, None, None]
    low = np.arange(16)[None, None, :, None]
    i = np.arange(TU)[None, None, None, :]
    cos, sin = turn(i * (16 * g + low + BANDS * high), GRID)
    parts = np.stack([cos, -sin], axis=4)
    full = parts[..., None] * np.eye(16)[None, None, :, None, None, :]
    return full.reshape(groups, TU * 16, TU * 2 * 16).astype(BF16)


def grid_tiles(vis_ref, ku_ref, kv_ref, ou_ref, ov_ref, ku_wide, kv_wide, tile_ref):
    taps, blocks = ku_ref.shape[:2]
    ku_wide[...] = ku_ref[...].astype(jnp.float32)
    kv_wide[...] = kv_ref[...].astype(jnp.float32)

    def one(b, carry):
        d_u = lax.broadcasted_iota(jnp.int32, (TU, TV), 0) - ou_ref[0, pl.ds(b, 1), :]
        d_v = lax.broadcasted_iota(jnp.int32, (TV, TV), 0) - ov_ref[0, pl.ds(b, 1), :]
        vis = vis_ref[0, b].astype(jnp.float32)
        spread_u = jnp.zeros((TU, TV), jnp.float32)
        spread_v = jnp.zeros((TV, TV), jnp.float32)
        for t in range(taps):
            spread_u = jnp.where(d_u == t, ku_wide[t, pl.ds(b, 1), :], spread_u)
            spread_v = jnp.where(d_v == t, kv_wide[t, pl.ds(b, 1), :], spread_v)
        left = jnp.concatenate([vis[0:1] * spread_u, vis[1:2] * spread_u], axis=0)
        tile = lax.dot_general(
            left.astype(jnp.bfloat16),
            spread_v.astype(jnp.bfloat16),
            (((1,), (1,)), ((), ())),
            preferred_element_type=jnp.float32,
        )
        for i in range(TU):
            tile_ref[i, pl.ds(b, 1), :] = tile[i : i + 1]
            tile_ref[TU + i, pl.ds(b, 1), :] = tile[TU + i : TU + i + 1]
        return carry

    lax.fori_loop(0, blocks, one, 0, unroll=4)


def image_kernel(
    freq_count,
    row_count,
    vis_ref,
    ku_ref,
    kv_ref,
    ou_ref,
    ov_ref,
    ids_ref,
    x_ref,
    phase_table_ref,
    band_table_ref,
    tile_table_hbm,
    inner_hbm,
    out_ref,
    ku_wide,
    kv_wide,
    grid_ref,
    tiles_ref,
    tile_table_ref,
    inner_ref,
    factor_ref,
    phase_ref,
    mid_ref,
    send_ref,
    recv_ref,
    x_send_ref,
    x_recv_ref,
    table_sem,
    swap_sem,
    row_send,
    row_recv,
    core_send,
    core_recv,
    send_sem,
    recv_sem,
    x_send_sem,
    x_recv_sem,
):
    me, row = lax.axis_index("freq"), lax.axis_index("row")
    block_count = ku_ref.shape[1]
    blocks = row_count * block_count
    chunks, chunk = send_ref.shape[1], send_ref.shape[4]
    share = TU // freq_count
    half = freq_count // 2
    first_of_half = me // half * half
    partner = lax.rem(me + half, freq_count)
    group = [first_of_half + lax.rem(me - first_of_half + d, half) for d in range(1, half)]
    pairs = row_count // 2
    pair, sub = row // 2, lax.rem(row, 2)
    sibling = pair * 2 + 1 - sub
    targets = [lax.rem(pair + d, pairs) * 2 + sub for d in range(1, pairs)]
    sources = [lax.rem(pair + pairs - d, pairs) * 2 + sub for d in range(1, pairs)]
    everyone = [{"freq": f} for f in [partner] + group] + [{"row": r} for r in [sibling] + targets]

    barrier = pltpu.get_barrier_semaphore()
    for device in everyone:
        pl.semaphore_signal(
            barrier, inc=1, device_id=device, device_id_type=pl.DeviceIdType.MESH
        )
    inner_rows = pl.ds(first_of_half * share * 16, TU // 2 * 16)
    tables = [
        pltpu.make_async_copy(tile_table_hbm.at[row], tile_table_ref, table_sem.at[0]),
        pltpu.make_async_copy(inner_hbm.at[:, inner_rows, :], inner_ref, table_sem.at[1]),
    ]
    for copy in tables:
        copy.start()

    grid_tiles(vis_ref, ku_ref, kv_ref, ou_ref, ov_ref, ku_wide, kv_wide, grid_ref)
    for i in range(TU):
        rows = slice(i * block_count, (i + 1) * block_count)
        tiles_ref[0, row, rows, :TV] = grid_ref[i].astype(jnp.bfloat16)
        tiles_ref[0, row, rows, TV:] = grid_ref[TU + i].astype(jnp.bfloat16)
    meta_rows = slice(TU * block_count, TU * block_count + 16)
    x = x_ref[...]
    x_main = x.astype(jnp.bfloat16).astype(jnp.float32)
    x_next = (x - x_main).astype(jnp.bfloat16).astype(jnp.float32)
    x_last = x - x_main - x_next
    line = lax.broadcasted_iota(jnp.int32, (16, 2 * TV), 0)
    meta = jnp.where(line == 2, x_main, ids_ref[...])
    meta = jnp.where(line == 3, x_next, jnp.where(line == 4, x_last, meta))
    tiles_ref[0, row, meta_rows, :] = meta.astype(jnp.bfloat16)

    def remote(src, dst, send, recv, device):
        copy = pltpu.make_async_remote_copy(
            src_ref=src,
            dst_ref=dst,
            send_sem=send,
            recv_sem=recv,
            device_id=device,
            device_id_type=pl.DeviceIdType.MESH,
        )
        copy.start()
        return copy

    def to_rows(c):
        own = tiles_ref.at[c, row]
        direct = [
            remote(own, own, row_send.at[c, n], row_recv.at[c, n], {"row": target})
            for n, target in enumerate(targets)
        ]
        return direct, [
            remote(own, own, core_send.at[c, 0], core_recv.at[c, 0], {"row": sibling})
        ]

    def forward(c, direct):
        passed = []
        for n, source in enumerate(sources):
            direct[n].wait_recv()
            block = tiles_ref.at[c, source]
            passed.append(
                remote(
                    block,
                    block,
                    core_send.at[c, n + 1],
                    core_recv.at[c, n + 1],
                    {"row": sibling},
                )
            )
        return passed

    pl.semaphore_wait(barrier, len(everyone))
    swap = remote(
        tiles_ref.at[0, row],
        tiles_ref.at[1, row],
        swap_sem.at[0],
        swap_sem.at[1],
        {"freq": partner},
    )
    direct_a, near_a = to_rows(0)
    near_a += forward(0, direct_a)
    swap.wait_recv()
    direct_b, near_b = to_rows(1)

    def x_of(c):
        meta = tiles_ref[c, row, meta_rows, :].astype(jnp.float32)
        return meta[2:3] + (meta[3:4] + meta[4:5])

    x_own = [x_of(0)[:, :chunk], x_of(1)[:, :chunk]]
    for c in range(2):
        x_send_ref[c * 8 : (c + 1) * 8, :] = jnp.broadcast_to(x_own[c], (8, chunk))
    x_copies = [
        remote(x_send_ref, x_recv_ref.at[n], x_send_sem.at[n], x_recv_sem.at[n], {"freq": peer})
        for n, peer in enumerate(group)
    ]
    for copy in near_a:
        copy.wait_recv()
    for copy in tables:
        copy.wait()

    def channel(c):
        for p in range(pairs):
            at = meta_rows.start
            ids = (
                tiles_ref[c, 2 * p, at : at + 16, :TV].astype(jnp.float32)
                + tiles_ref[c, 2 * p + 1, at : at + 16, :TV].astype(jnp.float32)
            )
            ids = ids.astype(jnp.int32)
            lanes = slice(p * TV, (p + 1) * TV)
            bands = lax.broadcasted_iota(jnp.int32, (BANDS, TV), 0) == ids[0:1]
            picked = jnp.dot(
                band_table_ref[...],
                bands.astype(jnp.float32).astype(jnp.bfloat16),
                preferred_element_type=jnp.float32,
            ).astype(jnp.bfloat16)
            imag_lanes = slice(blocks + p * TV, blocks + (p + 1) * TV)
            factor_ref[:BANDS, lanes] = picked[:BANDS]
            factor_ref[:BANDS, imag_lanes] = -picked[BANDS:]
            factor_ref[BANDS:, lanes] = picked[BANDS:]
            factor_ref[BANDS:, imag_lanes] = picked[:BANDS]
            cols = lax.broadcasted_iota(jnp.int32, (TILE_COLS, TV), 0) == ids[1:2]
            phase_ref[lanes, :] = lax.dot_general(
                cols.astype(jnp.float32).astype(jnp.bfloat16),
                phase_table_ref[...],
                (((0,), (0,)), ((), ())),
                preferred_element_type=jnp.float32,
            ).astype(jnp.bfloat16)

        copies = []
        for q in range(chunks):

            def first(i, carry):
                rows = pl.ds(pl.multiple_of(i * block_count, block_count), block_count)
                tiles = tiles_ref[c, :, rows, :].reshape(blocks, 2 * TV)
                cols = jnp.dot(tiles, tile_table_ref[q], preferred_element_type=jnp.float32)
                cols = cols.astype(jnp.bfloat16)
                real, imag = cols[:, :chunk], cols[:, chunk:]
                cos, sin = phase_ref[:, :chunk], phase_ref[:, chunk:]
                turned = jnp.concatenate(
                    [real * cos - imag * sin, real * sin + imag * cos], axis=0
                )
                y = jnp.dot(factor_ref[...], turned, preferred_element_type=jnp.float32)
                mid_ref[pl.ds(2 * i, 2)] = y.astype(jnp.bfloat16).reshape(2, BANDS, chunk)
                return carry

            lax.fori_loop(0, TU, first, 0, unroll=4)

            def second(g, carry):
                rows = pl.ds(pl.multiple_of(g * 16, 16), 16)
                y = mid_ref[:, rows, :].reshape(2 * TU * 16, chunk)
                z = jnp.dot(inner_ref[g], y, preferred_element_type=jnp.float32)
                send_ref[c, q, :, rows, :] = z.astype(jnp.bfloat16).reshape(TU // 2, 16, chunk)
                return carry

            lax.fori_loop(0, BANDS // 16, second, 0, unroll=4)
            for n, peer in enumerate(group):
                copies.append(
                    remote(
                        send_ref.at[c, q, pl.ds((peer - first_of_half) * share, share)],
                        recv_ref.at[c, q, n],
                        send_sem.at[c, q, n],
                        recv_sem.at[c, q, n],
                        {"freq": peer},
                    )
                )
        return copies

    images = channel(0)
    near_b += forward(1, direct_b)
    for copy in near_b:
        copy.wait_recv()
    images += channel(1)

    for copy in x_copies:
        copy.wait()
    for copy in direct_a + direct_b + near_a + near_b + [swap]:
        copy.wait_send()
    step = 32
    for q in range(chunks):
        for c in range(2):
            for n in range(half - 1):
                images[(c * chunks + q) * (half - 1) + n].wait()

        def combine(at, carry):
            h = at // (BANDS // step)
            rows = pl.ds(pl.multiple_of(at % (BANDS // step) * step, step), step)
            total = [jnp.zeros((step, chunk), jnp.float32) for _ in range(3)]
            for c in range(2):
                own_at = (me - first_of_half) * share + h
                terms = [(x_own[c], send_ref[c, q, own_at, rows, :])]
                for n in range(half - 1):
                    x_other = x_recv_ref[n, c * 8 : c * 8 + 1, :]
                    terms.append((x_other, recv_ref[c, q, n, h, rows, :]))
                for x_term, image in terms:
                    image = image.astype(jnp.float32)
                    total[0] += image
                    total[1] += x_term * image
                    total[2] += (x_term * x_term) * image
            for k in range(3):
                out_ref[k, h, rows, q * chunk : (q + 1) * chunk] = total[k].astype(jnp.bfloat16)
            return carry

        lax.fori_loop(0, share * (BANDS // step), combine, 0)


def shards(
    vis_values, kernel_u, kernel_v, offset_u, offset_v, block_owner, tile_slot, channel_freq
):
    row_count = lax.axis_size("row")
    freq_count = lax.axis_size("freq")
    blocks = vis_values.shape[1]
    vis_count = vis_values.shape[3]
    taps = kernel_u.shape[2]
    width = GRID // row_count
    tiles_slab = GRID // row_count // TU * TILE_COLS
    vmem = pl.BlockSpec(memory_space=pltpu.VMEM)
    chunk = min(256, width)
    chunks = width // chunk
    others = freq_count // 2 - 1
    share = TU // freq_count
    pairs = row_count // 2
    total_blocks = row_count * blocks

    tile = block_owner[0, :, 0] * tiles_slab + tile_slot[0]
    ids = jnp.stack([tile // TILE_COLS, tile % TILE_COLS]).astype(jnp.float32)
    odd = lax.axis_index("row") % 2
    ids = jnp.concatenate([jnp.where(odd == 0, ids, 0.0), jnp.where(odd == 1, ids, 0.0)], axis=1)
    ids = jnp.pad(ids, ((0, 14), (0, 2 * TV - 2 * blocks)))
    x = jnp.broadcast_to((channel_freq - 1.284) / 0.428, (16, 2 * TV))
    scale = 1.0 / math.sqrt(blocks * row_count * vis_count)
    dma = pltpu.SemaphoreType.DMA
    with jax.named_scope("image"):
        image = pl.pallas_call(
            partial(image_kernel, freq_count, row_count),
            out_shape=jax.ShapeDtypeStruct((3, share, BANDS, width), jnp.bfloat16),
            in_specs=[vmem] * 9 + [pl.BlockSpec(memory_space=pl.ANY)] * 2,
            out_specs=vmem,
            scratch_shapes=[
                pltpu.VMEM((taps, blocks, TV), jnp.float32),
                pltpu.VMEM((taps, blocks, TV), jnp.float32),
                pltpu.VMEM((2 * TU, blocks, TV), jnp.float32),
                pltpu.VMEM((2, row_count, TU * blocks + 16, 2 * TV), jnp.bfloat16),
                pltpu.VMEM((chunks, 2 * TV, 2 * chunk), jnp.bfloat16),
                pltpu.VMEM((BANDS // 16, TU // 2 * 16, 2 * TU * 16), jnp.bfloat16),
                pltpu.VMEM((2 * BANDS, 2 * total_blocks), jnp.bfloat16),
                pltpu.VMEM((total_blocks, 2 * chunk), jnp.bfloat16),
                pltpu.VMEM((2 * TU, BANDS, chunk), jnp.bfloat16),
                pltpu.VMEM((2, chunks, TU // 2, BANDS, chunk), jnp.bfloat16),
                pltpu.VMEM((2, chunks, others, share, BANDS, chunk), jnp.bfloat16),
                pltpu.VMEM((16, chunk), jnp.float32),
                pltpu.VMEM((others, 16, chunk), jnp.float32),
                dma((2,)),
                dma((2,)),
                dma((2, pairs - 1)),
                dma((2, pairs - 1)),
                dma((2, pairs)),
                dma((2, pairs)),
                dma((2, chunks, others)),
                dma((2, chunks, others)),
                dma((others,)),
                dma((others,)),
            ],
            compiler_params=pltpu.CompilerParams(
                vmem_limit_bytes=VMEM_LIMIT, collective_id=0, has_side_effects=True
            ),
        )(
            vis_values,
            kernel_u[0].transpose(1, 0, 2),
            kernel_v[0].transpose(1, 0, 2),
            offset_u,
            offset_v,
            ids,
            x,
            phase_table(chunk),
            band_table(scale),
            tile_tables(row_count, chunk),
            inner_table(),
        )
    return image.reshape(3, GRID // freq_count, width)


def solution(mesh):
    return jax.shard_map(
        shards,
        mesh=mesh,
        in_specs=(
            P("freq", "row", None, None),
            P("freq", "row", None, None),
            P("freq", "row", None, None),
            P("freq", "row", None),
            P("freq", "row", None),
            P("freq", "row", None),
            P("freq", "row"),
            P("freq"),
        ),
        out_specs=P(None, "freq", "row"),
        check_vma=False,
    )
```

```python
from functools import partial
import math

import jax
import jax.numpy as jnp
import ml_dtypes
import numpy as np
from jax import lax
from jax.experimental import pallas as pl
from jax.experimental.pallas import tpu as pltpu
from jax.sharding import PartitionSpec as P

GRID = 4096
TU = 16
TV = 128
BANDS = GRID // TU
TILE_COLS = GRID // TV
BF16 = ml_dtypes.bfloat16
VMEM_LIMIT = 56 * 1024 * 1024


def turn(index, length):
    angle = 2.0 * np.pi * (index % length) / length
    return np.cos(angle), np.sin(angle)


def tile_tables(row_count, chunk):
    j = np.arange(TV)[:, None]
    m = np.arange(GRID)[None, :]
    cos, sin = turn(j * m, GRID)
    cos = cos.reshape(TV, row_count, -1, chunk).transpose(1, 2, 0, 3)
    sin = sin.reshape(TV, row_count, -1, chunk).transpose(1, 2, 0, 3)
    top = np.concatenate([cos, sin], axis=3)
    low = np.concatenate([-sin, cos], axis=3)
    return np.concatenate([top, low], axis=2).astype(BF16)


def phase_table(chunk):
    cos, sin = turn(np.arange(TILE_COLS)[:, None] * np.arange(chunk)[None, :], TILE_COLS)
    return np.concatenate([cos, sin], axis=1).astype(BF16)


def band_table(scale):
    index = np.arange(BANDS)
    cos, sin = turn(index[:, None] * index[None, :], BANDS)
    return (np.concatenate([cos, sin], axis=0) * scale).astype(BF16)


def inner_table():
    groups = BANDS // 16
    g = np.arange(groups)[:, None, None, None]
    high = np.arange(TU)[None, :, None, None]
    low = np.arange(16)[None, None, :, None]
    i = np.arange(TU)[None, None, None, :]
    cos, sin = turn(i * (16 * g + low + BANDS * high), GRID)
    parts = np.stack([cos, -sin], axis=4)
    full = parts[..., None] * np.eye(16)[None, None, :, None, None, :]
    return full.reshape(groups, TU * 16, TU * 2 * 16).astype(BF16)


def grid_tiles(first, count, vis_ref, ou_ref, ov_ref, ku_wide, kv_wide, tile_ref):
    taps = ku_wide.shape[0]

    def one(b, carry):
        d_u = lax.broadcasted_iota(jnp.int32, (TU, TV), 0) - ou_ref[0, pl.ds(b, 1), :]
        d_v = lax.broadcasted_iota(jnp.int32, (TV, TV), 0) - ov_ref[0, pl.ds(b, 1), :]
        vis = vis_ref[0, b].astype(jnp.float32)
        spread_u = jnp.zeros((TU, TV), jnp.float32)
        spread_v = jnp.zeros((TV, TV), jnp.float32)
        for t in range(taps):
            spread_u = jnp.where(d_u == t, ku_wide[t, pl.ds(b, 1), :], spread_u)
            spread_v = jnp.where(d_v == t, kv_wide[t, pl.ds(b, 1), :], spread_v)
        left = jnp.concatenate([vis[0:1] * spread_u, vis[1:2] * spread_u], axis=0)
        tile = lax.dot_general(
            left.astype(jnp.bfloat16),
            spread_v.astype(jnp.bfloat16),
            (((1,), (1,)), ((), ())),
            preferred_element_type=jnp.float32,
        )
        for i in range(TU):
            tile_ref[i, pl.ds(b, 1), :] = tile[i : i + 1]
            tile_ref[TU + i, pl.ds(b, 1), :] = tile[TU + i : TU + i + 1]
        return carry

    lax.fori_loop(first, first + count, one, 0, unroll=4)


def image_kernel(
    freq_count,
    row_count,
    vis_ref,
    ku_ref,
    kv_ref,
    ou_ref,
    ov_ref,
    ids_ref,
    x_ref,
    phase_table_ref,
    band_table_ref,
    tile_table_hbm,
    inner_hbm,
    out_ref,
    ku_wide,
    kv_wide,
    grid_ref,
    tiles_ref,
    tile_table_ref,
    inner_ref,
    factor_ref,
    phase_ref,
    mid_ref,
    send_ref,
    recv_ref,
    x_send_ref,
    x_recv_ref,
    table_sem,
    swap_sem,
    row_send,
    row_recv,
    core_send,
    core_recv,
    send_sem,
    recv_sem,
    x_send_sem,
    x_recv_sem,
):
    me, row = lax.axis_index("freq"), lax.axis_index("row")
    block_count = ku_ref.shape[1]
    blocks = row_count * block_count
    chunks, chunk = send_ref.shape[1], send_ref.shape[4]
    share = TU // freq_count
    half = freq_count // 2
    first_of_half = me // half * half
    partner = lax.rem(me + half, freq_count)
    group = [first_of_half + lax.rem(me - first_of_half + d, half) for d in range(1, half)]
    pairs = row_count // 2
    pair, sub = row // 2, lax.rem(row, 2)
    sibling = pair * 2 + 1 - sub
    tree = pairs == 4
    if tree:
        y, x = pair // 2, lax.rem(pair, 2)
        sources = [
            (y * 2 + 1 - x) * 2 + sub,
            ((1 - y) * 2 + x) * 2 + sub,
            ((1 - y) * 2 + 1 - x) * 2 + sub,
        ]
        targets = sources[:2]
    else:
        sources = [lax.rem(pair + pairs - d, pairs) * 2 + sub for d in range(1, pairs)]
        targets = [lax.rem(pair + d, pairs) * 2 + sub for d in range(1, pairs)]
    everyone = [{"freq": f} for f in [partner] + group] + [{"row": r} for r in [sibling] + targets]

    barrier = pltpu.get_barrier_semaphore()
    for device in everyone:
        pl.semaphore_signal(
            barrier, inc=1, device_id=device, device_id_type=pl.DeviceIdType.MESH
        )
    inner_rows = pl.ds(first_of_half * share * 16, TU // 2 * 16)
    tables = [
        pltpu.make_async_copy(tile_table_hbm.at[row], tile_table_ref, table_sem.at[0]),
        pltpu.make_async_copy(inner_hbm.at[:, inner_rows, :], inner_ref, table_sem.at[1]),
    ]
    for copy in tables:
        copy.start()

    part_blocks = block_count // 2

    def grid_part(p):
        first = p * part_blocks
        grid_tiles(first, part_blocks, vis_ref, ou_ref, ov_ref, ku_wide, kv_wide, grid_ref)
        for i in range(TU):
            rows = slice(i * part_blocks, (i + 1) * part_blocks)
            taken = slice(first, first + part_blocks)
            tiles_ref[0, row, p, rows, :TV] = grid_ref[i, taken].astype(jnp.bfloat16)
            tiles_ref[0, row, p, rows, TV:] = grid_ref[TU + i, taken].astype(jnp.bfloat16)

    ku_wide[...] = ku_ref[...].astype(jnp.float32)
    kv_wide[...] = kv_ref[...].astype(jnp.float32)
    grid_part(0)
    meta_rows = slice(TU * part_blocks, TU * part_blocks + 16)
    x = x_ref[...]
    x_main = x.astype(jnp.bfloat16).astype(jnp.float32)
    x_next = (x - x_main).astype(jnp.bfloat16).astype(jnp.float32)
    x_last = x - x_main - x_next
    line = lax.broadcasted_iota(jnp.int32, (16, 2 * TV), 0)
    meta = jnp.where(line == 2, x_main, ids_ref[...])
    meta = jnp.where(line == 3, x_next, jnp.where(line == 4, x_last, meta))
    for p in range(2):
        tiles_ref[0, row, p, meta_rows, :] = meta.astype(jnp.bfloat16)

    def remote(src, dst, send, recv, device):
        copy = pltpu.make_async_remote_copy(
            src_ref=src,
            dst_ref=dst,
            send_sem=send,
            recv_sem=recv,
            device_id=device,
            device_id_type=pl.DeviceIdType.MESH,
        )
        copy.start()
        return copy

    direct, near = {}, {}

    def to_rows(c, p):
        own = tiles_ref.at[c, row, p]
        for n, target in enumerate(targets):
            direct[c, n, p] = remote(
                own, own, row_send.at[c, n, p], row_recv.at[c, n, p], {"row": target}
            )
        near[c, 0, p] = remote(
            own, own, core_send.at[c, 0, p], core_recv.at[c, 0, p], {"row": sibling}
        )

    def to_sibling(c, n, p):
        direct[c, n, p].wait_recv()
        block = tiles_ref.at[c, sources[n], p]
        near[c, n + 1, p] = remote(
            block, block, core_send.at[c, n + 1, p], core_recv.at[c, n + 1, p], {"row": sibling}
        )

    def relay(c, p):
        for n in range(len(targets)):
            to_sibling(c, n, p)
            if tree and n == p:
                block = tiles_ref.at[c, sources[n], p]
                direct[c, 2, p] = remote(
                    block, block, row_send.at[c, 2, p], row_recv.at[c, 2, p],
                    {"row": targets[1 - n]},
                )

    def relay_last(c):
        if tree:
            for p in range(2):
                to_sibling(c, 2, p)

    def swap_part(p):
        return remote(
            tiles_ref.at[0, row, p],
            tiles_ref.at[1, row, p],
            swap_sem.at[0, p],
            swap_sem.at[1, p],
            {"freq": partner},
        )

    def all_near(c):
        for n in range(pairs):
            for p in range(2):
                near[c, n, p].wait_recv()

    pl.semaphore_wait(barrier, len(everyone))
    swaps = [swap_part(0)]
    to_rows(0, 0)
    grid_part(1)
    swaps.append(swap_part(1))
    to_rows(0, 1)
    relay(0, 0)
    relay(0, 1)
    swaps[0].wait_recv()
    to_rows(1, 0)
    relay_last(0)
    swaps[1].wait_recv()
    to_rows(1, 1)

    def x_of(c):
        meta = tiles_ref[c, row, 0, meta_rows, :].astype(jnp.float32)
        return meta[2:3] + (meta[3:4] + meta[4:5])

    x_own = [x_of(0)[:, :chunk], x_of(1)[:, :chunk]]
    for c in range(2):
        x_send_ref[c * 8 : (c + 1) * 8, :] = jnp.broadcast_to(x_own[c], (8, chunk))
    x_copies = [
        remote(x_send_ref, x_recv_ref.at[n], x_send_sem.at[n], x_recv_sem.at[n], {"freq": peer})
        for n, peer in enumerate(group)
    ]
    all_near(0)
    for copy in tables:
        copy.wait()

    def channel(c, hooks):
        for p in range(pairs):
            at = meta_rows.start
            ids = (
                tiles_ref[c, 2 * p, 0, at : at + 16, :TV].astype(jnp.float32)
                + tiles_ref[c, 2 * p + 1, 0, at : at + 16, :TV].astype(jnp.float32)
            )
            ids = ids.astype(jnp.int32)
            lanes = slice(p * TV, (p + 1) * TV)
            bands = lax.broadcasted_iota(jnp.int32, (BANDS, TV), 0) == ids[0:1]
            picked = jnp.dot(
                band_table_ref[...],
                bands.astype(jnp.float32).astype(jnp.bfloat16),
                preferred_element_type=jnp.float32,
            ).astype(jnp.bfloat16)
            imag_lanes = slice(blocks + p * TV, blocks + (p + 1) * TV)
            factor_ref[:BANDS, lanes] = picked[:BANDS]
            factor_ref[:BANDS, imag_lanes] = -picked[BANDS:]
            factor_ref[BANDS:, lanes] = picked[BANDS:]
            factor_ref[BANDS:, imag_lanes] = picked[:BANDS]
            cols = lax.broadcasted_iota(jnp.int32, (TILE_COLS, TV), 0) == ids[1:2]
            phase_ref[lanes, :] = lax.dot_general(
                cols.astype(jnp.float32).astype(jnp.bfloat16),
                phase_table_ref[...],
                (((0,), (0,)), ((), ())),
                preferred_element_type=jnp.float32,
            ).astype(jnp.bfloat16)

        copies = []
        for q in range(chunks):

            def first(i, carry):
                rows = pl.ds(pl.multiple_of(i * part_blocks, part_blocks), part_blocks)
                tiles = tiles_ref[c, :, :, rows, :].reshape(blocks, 2 * TV)
                cols = jnp.dot(tiles, tile_table_ref[q], preferred_element_type=jnp.float32)
                cols = cols.astype(jnp.bfloat16)
                real, imag = cols[:, :chunk], cols[:, chunk:]
                cos, sin = phase_ref[:, :chunk], phase_ref[:, chunk:]
                turned = jnp.concatenate(
                    [real * cos - imag * sin, real * sin + imag * cos], axis=0
                )
                y = jnp.dot(factor_ref[...], turned, preferred_element_type=jnp.float32)
                mid_ref[pl.ds(2 * i, 2)] = y.astype(jnp.bfloat16).reshape(2, BANDS, chunk)
                return carry

            lax.fori_loop(0, TU, first, 0, unroll=4)
            if q == 0:
                hooks[0]()

            def second(g, carry):
                rows = pl.ds(pl.multiple_of(g * 16, 16), 16)
                y = mid_ref[:, rows, :].reshape(2 * TU * 16, chunk)
                z = jnp.dot(inner_ref[g], y, preferred_element_type=jnp.float32)
                send_ref[c, q, :, rows, :] = z.astype(jnp.bfloat16).reshape(TU // 2, 16, chunk)
                return carry

            lax.fori_loop(0, BANDS // 16, second, 0, unroll=4)
            for n, peer in enumerate(group):
                copies.append(
                    remote(
                        send_ref.at[c, q, pl.ds((peer - first_of_half) * share, share)],
                        recv_ref.at[c, q, n],
                        send_sem.at[c, q, n],
                        recv_sem.at[c, q, n],
                        {"freq": peer},
                    )
                )
            if q == 0:
                hooks[1]()
        return copies

    images = channel(0, (lambda: relay(1, 0), lambda: relay(1, 1)))
    relay_last(1)
    all_near(1)
    images += channel(1, (lambda: None, lambda: None))

    for copy in x_copies:
        copy.wait()
    for copy in swaps + list(direct.values()) + list(near.values()):
        copy.wait_send()
    step = 32
    for q in range(chunks):
        for c in range(2):
            for n in range(half - 1):
                images[(c * chunks + q) * (half - 1) + n].wait()

        def combine(at, carry):
            h = at // (BANDS // step)
            rows = pl.ds(pl.multiple_of(at % (BANDS // step) * step, step), step)
            total = [jnp.zeros((step, chunk), jnp.float32) for _ in range(3)]
            for c in range(2):
                own_at = (me - first_of_half) * share + h
                terms = [(x_own[c], send_ref[c, q, own_at, rows, :])]
                for n in range(half - 1):
                    x_other = x_recv_ref[n, c * 8 : c * 8 + 1, :]
                    terms.append((x_other, recv_ref[c, q, n, h, rows, :]))
                for x_term, image in terms:
                    image = image.astype(jnp.float32)
                    total[0] += image
                    total[1] += x_term * image
                    total[2] += (x_term * x_term) * image
            for k in range(3):
                out_ref[k, h, rows, q * chunk : (q + 1) * chunk] = total[k].astype(jnp.bfloat16)
            return carry

        lax.fori_loop(0, share * (BANDS // step), combine, 0)


def shards(
    vis_values, kernel_u, kernel_v, offset_u, offset_v, block_owner, tile_slot, channel_freq
):
    row_count = lax.axis_size("row")
    freq_count = lax.axis_size("freq")
    blocks = vis_values.shape[1]
    vis_count = vis_values.shape[3]
    taps = kernel_u.shape[2]
    width = GRID // row_count
    tiles_slab = GRID // row_count // TU * TILE_COLS
    vmem = pl.BlockSpec(memory_space=pltpu.VMEM)
    chunk = min(256, width)
    chunks = width // chunk
    others = freq_count // 2 - 1
    share = TU // freq_count
    pairs = row_count // 2
    total_blocks = row_count * blocks

    tile = block_owner[0, :, 0] * tiles_slab + tile_slot[0]
    ids = jnp.stack([tile // TILE_COLS, tile % TILE_COLS]).astype(jnp.float32)
    odd = lax.axis_index("row") % 2
    ids = jnp.concatenate([jnp.where(odd == 0, ids, 0.0), jnp.where(odd == 1, ids, 0.0)], axis=1)
    ids = jnp.pad(ids, ((0, 14), (0, 2 * TV - 2 * blocks)))
    x = jnp.broadcast_to((channel_freq - 1.284) / 0.428, (16, 2 * TV))
    scale = 1.0 / math.sqrt(blocks * row_count * vis_count)
    dma = pltpu.SemaphoreType.DMA
    with jax.named_scope("image"):
        image = pl.pallas_call(
            partial(image_kernel, freq_count, row_count),
            out_shape=jax.ShapeDtypeStruct((3, share, BANDS, width), jnp.bfloat16),
            in_specs=[vmem] * 9 + [pl.BlockSpec(memory_space=pl.ANY)] * 2,
            out_specs=vmem,
            scratch_shapes=[
                pltpu.VMEM((taps, blocks, TV), jnp.float32),
                pltpu.VMEM((taps, blocks, TV), jnp.float32),
                pltpu.VMEM((2 * TU, blocks, TV), jnp.float32),
                pltpu.VMEM((2, row_count, 2, TU * blocks // 2 + 16, 2 * TV), jnp.bfloat16),
                pltpu.VMEM((chunks, 2 * TV, 2 * chunk), jnp.bfloat16),
                pltpu.VMEM((BANDS // 16, TU // 2 * 16, 2 * TU * 16), jnp.bfloat16),
                pltpu.VMEM((2 * BANDS, 2 * total_blocks), jnp.bfloat16),
                pltpu.VMEM((total_blocks, 2 * chunk), jnp.bfloat16),
                pltpu.VMEM((2 * TU, BANDS, chunk), jnp.bfloat16),
                pltpu.VMEM((2, chunks, TU // 2, BANDS, chunk), jnp.bfloat16),
                pltpu.VMEM((2, chunks, others, share, BANDS, chunk), jnp.bfloat16),
                pltpu.VMEM((16, chunk), jnp.float32),
                pltpu.VMEM((others, 16, chunk), jnp.float32),
                dma((2,)),
                dma((2, 2)),
                dma((2, pairs - 1, 2)),
                dma((2, pairs - 1, 2)),
                dma((2, pairs, 2)),
                dma((2, pairs, 2)),
                dma((2, chunks, others)),
                dma((2, chunks, others)),
                dma((others,)),
                dma((others,)),
            ],
            compiler_params=pltpu.CompilerParams(
                vmem_limit_bytes=VMEM_LIMIT, collective_id=0, has_side_effects=True
            ),
        )(
            vis_values,
            kernel_u[0].transpose(1, 0, 2),
            kernel_v[0].transpose(1, 0, 2),
            offset_u,
            offset_v,
            ids,
            x,
            phase_table(chunk),
            band_table(scale),
            tile_tables(row_count, chunk),
            inner_table(),
        )
    return image.reshape(3, GRID // freq_count, width)


def solution(mesh):
    return jax.shard_map(
        shards,
        mesh=mesh,
        in_specs=(
            P("freq", "row", None, None),
            P("freq", "row", None, None),
            P("freq", "row", None, None),
            P("freq", "row", None),
            P("freq", "row", None),
            P("freq", "row", None),
            P("freq", "row"),
            P("freq"),
        ),
        out_specs=P(None, "freq", "row"),
        check_vma=False,
    )
```

```python
from functools import partial
import math

import jax
import jax.numpy as jnp
import ml_dtypes
import numpy as np
from jax import lax
from jax.experimental import pallas as pl
from jax.experimental.pallas import tpu as pltpu
from jax.sharding import PartitionSpec as P

GRID = 4096
TU = 16
TV = 128
BANDS = GRID // TU
TILE_COLS = GRID // TV
BF16 = ml_dtypes.bfloat16
VMEM_LIMIT = 56 * 1024 * 1024


def turn(index, length):
    angle = 2.0 * np.pi * (index % length) / length
    return np.cos(angle), np.sin(angle)


def tile_tables(row_count, chunk):
    j = np.arange(TV)[:, None]
    m = np.arange(GRID)[None, :]
    cos, sin = turn(j * m, GRID)
    cos = cos.reshape(TV, row_count, -1, chunk).transpose(1, 2, 0, 3)
    sin = sin.reshape(TV, row_count, -1, chunk).transpose(1, 2, 0, 3)
    top = np.concatenate([cos, sin], axis=3)
    low = np.concatenate([-sin, cos], axis=3)
    return np.concatenate([top, low], axis=2).astype(BF16)


def phase_table(chunk):
    cos, sin = turn(np.arange(TILE_COLS)[:, None] * np.arange(chunk)[None, :], TILE_COLS)
    return np.concatenate([cos, sin], axis=1).astype(BF16)


def band_table(scale):
    index = np.arange(BANDS)
    cos, sin = turn(index[:, None] * index[None, :], BANDS)
    return (np.concatenate([cos, sin], axis=0) * scale).astype(BF16)


def inner_table():
    groups = BANDS // 16
    g = np.arange(groups)[:, None, None, None]
    high = np.arange(TU)[None, :, None, None]
    low = np.arange(16)[None, None, :, None]
    i = np.arange(TU)[None, None, None, :]
    cos, sin = turn(i * (16 * g + low + BANDS * high), GRID)
    parts = np.stack([cos, -sin], axis=4)
    full = parts[..., None] * np.eye(16)[None, None, :, None, None, :]
    return full.reshape(groups, TU * 16, TU * 2 * 16).astype(BF16)


def grid_tiles(first, count, vis_ref, ou_ref, ov_ref, ku_wide, kv_wide, tile_ref):
    taps = ku_wide.shape[0]

    def one(b, carry):
        d_u = lax.broadcasted_iota(jnp.int32, (TU, TV), 0) - ou_ref[0, pl.ds(b, 1), :]
        d_v = lax.broadcasted_iota(jnp.int32, (TV, TV), 0) - ov_ref[0, pl.ds(b, 1), :]
        vis = vis_ref[0, b].astype(jnp.float32)
        spread_u = jnp.zeros((TU, TV), jnp.float32)
        spread_v = jnp.zeros((TV, TV), jnp.float32)
        for t in range(taps):
            spread_u = jnp.where(d_u == t, ku_wide[t, pl.ds(b, 1), :], spread_u)
            spread_v = jnp.where(d_v == t, kv_wide[t, pl.ds(b, 1), :], spread_v)
        left = jnp.concatenate([vis[0:1] * spread_u, vis[1:2] * spread_u], axis=0)
        tile = lax.dot_general(
            left.astype(jnp.bfloat16),
            spread_v.astype(jnp.bfloat16),
            (((1,), (1,)), ((), ())),
            preferred_element_type=jnp.float32,
        )
        for i in range(TU):
            tile_ref[i, pl.ds(b, 1), :] = tile[i : i + 1]
            tile_ref[TU + i, pl.ds(b, 1), :] = tile[TU + i : TU + i + 1]
        return carry

    lax.fori_loop(first, first + count, one, 0, unroll=4)


def image_kernel(
    freq_count,
    row_count,
    vis_ref,
    ku_ref,
    kv_ref,
    ou_ref,
    ov_ref,
    ids_ref,
    x_ref,
    phase_table_ref,
    band_table_ref,
    tile_table_hbm,
    inner_hbm,
    out_ref,
    ku_wide,
    kv_wide,
    grid_ref,
    tiles_ref,
    tile_table_ref,
    inner_ref,
    factor_ref,
    phase_ref,
    mid_ref,
    send_ref,
    recv_ref,
    x_send_ref,
    x_recv_ref,
    table_sem,
    swap_sem,
    row_send,
    row_recv,
    core_send,
    core_recv,
    send_sem,
    recv_sem,
    x_send_sem,
    x_recv_sem,
):
    me, row = lax.axis_index("freq"), lax.axis_index("row")
    block_count = ku_ref.shape[1]
    blocks = row_count * block_count
    chunks, chunk = send_ref.shape[1], send_ref.shape[4]
    share = TU // freq_count
    half = freq_count // 2
    first_of_half = me // half * half
    partner = lax.rem(me + half, freq_count)
    group = [first_of_half + lax.rem(me - first_of_half + d, half) for d in range(1, half)]
    pairs = row_count // 2
    pair, sub = row // 2, lax.rem(row, 2)
    sibling = pair * 2 + 1 - sub
    tree = pairs == 4
    if tree:
        y, x = pair // 2, lax.rem(pair, 2)
        sources = [
            (y * 2 + 1 - x) * 2 + sub,
            ((1 - y) * 2 + x) * 2 + sub,
            ((1 - y) * 2 + 1 - x) * 2 + sub,
        ]
        targets = sources[:2]
    else:
        sources = [lax.rem(pair + pairs - d, pairs) * 2 + sub for d in range(1, pairs)]
        targets = [lax.rem(pair + d, pairs) * 2 + sub for d in range(1, pairs)]
    everyone = [{"freq": f} for f in [partner] + group] + [{"row": r} for r in [sibling] + targets]

    barrier = pltpu.get_barrier_semaphore()
    for device in everyone:
        pl.semaphore_signal(
            barrier, inc=1, device_id=device, device_id_type=pl.DeviceIdType.MESH
        )
    inner_rows = pl.ds(first_of_half * share * 16, TU // 2 * 16)
    tables = [
        pltpu.make_async_copy(tile_table_hbm.at[row], tile_table_ref, table_sem.at[0]),
        pltpu.make_async_copy(inner_hbm.at[:, inner_rows, :], inner_ref, table_sem.at[1]),
    ]
    for copy in tables:
        copy.start()

    part_blocks = block_count // 2

    def grid_part(p):
        first = p * part_blocks
        grid_tiles(first, part_blocks, vis_ref, ou_ref, ov_ref, ku_wide, kv_wide, grid_ref)
        for i in range(TU):
            rows = slice(i * part_blocks, (i + 1) * part_blocks)
            taken = slice(first, first + part_blocks)
            tiles_ref[0, row, p, rows, :TV] = grid_ref[i, taken].astype(jnp.bfloat16)
            tiles_ref[0, row, p, rows, TV:] = grid_ref[TU + i, taken].astype(jnp.bfloat16)

    ku_wide[...] = ku_ref[...].astype(jnp.float32)
    kv_wide[...] = kv_ref[...].astype(jnp.float32)
    grid_part(0)
    meta_rows = slice(TU * part_blocks, TU * part_blocks + 16)
    x = x_ref[...]
    x_main = x.astype(jnp.bfloat16).astype(jnp.float32)
    x_next = (x - x_main).astype(jnp.bfloat16).astype(jnp.float32)
    x_last = x - x_main - x_next
    line = lax.broadcasted_iota(jnp.int32, (16, 2 * TV), 0)
    meta = jnp.where(line == 2, x_main, ids_ref[...])
    meta = jnp.where(line == 3, x_next, jnp.where(line == 4, x_last, meta))
    for p in range(2):
        tiles_ref[0, row, p, meta_rows, :] = meta.astype(jnp.bfloat16)

    def remote(src, dst, send, recv, device):
        copy = pltpu.make_async_remote_copy(
            src_ref=src,
            dst_ref=dst,
            send_sem=send,
            recv_sem=recv,
            device_id=device,
            device_id_type=pl.DeviceIdType.MESH,
        )
        copy.start()
        return copy

    direct, near = {}, {}

    def to_rows(c, p):
        own = tiles_ref.at[c, row, p]
        for n, target in enumerate(targets):
            direct[c, n, p] = remote(
                own, own, row_send.at[c, n, p], row_recv.at[c, n, p], {"row": target}
            )
        near[c, 0, p] = remote(
            own, own, core_send.at[c, 0, p], core_recv.at[c, 0, p], {"row": sibling}
        )

    def to_sibling(c, n, p):
        direct[c, n, p].wait_recv()
        block = tiles_ref.at[c, sources[n], p]
        near[c, n + 1, p] = remote(
            block, block, core_send.at[c, n + 1, p], core_recv.at[c, n + 1, p], {"row": sibling}
        )

    def relay(c, p):
        for n in range(len(targets)):
            to_sibling(c, n, p)
            if tree and n == p:
                block = tiles_ref.at[c, sources[n], p]
                direct[c, 2, p] = remote(
                    block, block, row_send.at[c, 2, p], row_recv.at[c, 2, p],
                    {"row": targets[1 - n]},
                )

    def relay_last(c):
        if tree:
            for p in range(2):
                to_sibling(c, 2, p)

    def swap_part(p):
        return remote(
            tiles_ref.at[0, row, p],
            tiles_ref.at[1, row, p],
            swap_sem.at[0, p],
            swap_sem.at[1, p],
            {"freq": partner},
        )

    def all_near(c):
        for n in range(pairs):
            for p in range(2):
                near[c, n, p].wait_recv()

    pl.semaphore_wait(barrier, len(everyone))
    swaps = [swap_part(0)]
    to_rows(0, 0)
    grid_part(1)
    swaps.append(swap_part(1))
    to_rows(0, 1)
    relay(0, 0)
    relay(0, 1)
    swaps[0].wait_recv()
    to_rows(1, 0)
    relay_last(0)
    swaps[1].wait_recv()
    to_rows(1, 1)

    def x_of(c):
        meta = tiles_ref[c, row, 0, meta_rows, :].astype(jnp.float32)
        return meta[2:3] + (meta[3:4] + meta[4:5])

    x_own = [x_of(0)[:, :chunk], x_of(1)[:, :chunk]]
    for c in range(2):
        x_send_ref[c * 8 : (c + 1) * 8, :] = jnp.broadcast_to(x_own[c], (8, chunk))
    x_copies = [
        remote(x_send_ref, x_recv_ref.at[n], x_send_sem.at[n], x_recv_sem.at[n], {"freq": peer})
        for n, peer in enumerate(group)
    ]
    all_near(0)
    for copy in tables:
        copy.wait()

    def channel(c, hooks):
        for p in range(pairs):
            at = meta_rows.start
            ids = (
                tiles_ref[c, 2 * p, 0, at : at + 16, :TV].astype(jnp.float32)
                + tiles_ref[c, 2 * p + 1, 0, at : at + 16, :TV].astype(jnp.float32)
            )
            ids = ids.astype(jnp.int32)
            lanes = slice(p * TV, (p + 1) * TV)
            bands = lax.broadcasted_iota(jnp.int32, (BANDS, TV), 0) == ids[0:1]
            picked = jnp.dot(
                band_table_ref[...],
                bands.astype(jnp.float32).astype(jnp.bfloat16),
                preferred_element_type=jnp.float32,
            ).astype(jnp.bfloat16)
            imag_lanes = slice(blocks + p * TV, blocks + (p + 1) * TV)
            factor_ref[:BANDS, lanes] = picked[:BANDS]
            factor_ref[:BANDS, imag_lanes] = -picked[BANDS:]
            factor_ref[BANDS:, lanes] = picked[BANDS:]
            factor_ref[BANDS:, imag_lanes] = picked[:BANDS]
            cols = lax.broadcasted_iota(jnp.int32, (TILE_COLS, TV), 0) == ids[1:2]
            phase_ref[lanes, :] = lax.dot_general(
                cols.astype(jnp.float32).astype(jnp.bfloat16),
                phase_table_ref[...],
                (((0,), (0,)), ((), ())),
                preferred_element_type=jnp.float32,
            ).astype(jnp.bfloat16)

        copies = []
        for q in range(chunks):

            def first(i, carry):
                rows = pl.ds(pl.multiple_of(i * part_blocks, part_blocks), part_blocks)
                tiles = tiles_ref[c, :, :, rows, :].reshape(blocks, 2 * TV)
                cols = jnp.dot(tiles, tile_table_ref[q], preferred_element_type=jnp.float32)
                cols = cols.astype(jnp.bfloat16)
                real, imag = cols[:, :chunk], cols[:, chunk:]
                cos, sin = phase_ref[:, :chunk], phase_ref[:, chunk:]
                turned = jnp.concatenate(
                    [real * cos - imag * sin, real * sin + imag * cos], axis=0
                )
                y = jnp.dot(factor_ref[...], turned, preferred_element_type=jnp.float32)
                mid_ref[pl.ds(2 * i, 2)] = y.astype(jnp.bfloat16).reshape(2, BANDS, chunk)
                return carry

            lax.fori_loop(0, TU, first, 0, unroll=8)
            if q == 0:
                hooks[0]()

            def second(g, carry):
                rows = pl.ds(pl.multiple_of(g * 16, 16), 16)
                y = mid_ref[:, rows, :].reshape(2 * TU * 16, chunk)
                z = jnp.dot(inner_ref[g], y, preferred_element_type=jnp.float32)
                send_ref[c, q, :, rows, :] = z.astype(jnp.bfloat16).reshape(TU // 2, 16, chunk)
                return carry

            lax.fori_loop(0, BANDS // 16, second, 0, unroll=8)
            for n, peer in enumerate(group):
                copies.append(
                    remote(
                        send_ref.at[c, q, pl.ds((peer - first_of_half) * share, share)],
                        recv_ref.at[c, q, n],
                        send_sem.at[c, q, n],
                        recv_sem.at[c, q, n],
                        {"freq": peer},
                    )
                )
            if q == 0:
                hooks[1]()
        return copies

    images = channel(0, (lambda: relay(1, 0), lambda: relay(1, 1)))
    relay_last(1)
    all_near(1)
    images += channel(1, (lambda: None, lambda: None))

    for copy in x_copies:
        copy.wait()
    for copy in swaps + list(direct.values()) + list(near.values()):
        copy.wait_send()
    step = 32
    for q in range(chunks):
        for c in range(2):
            for n in range(half - 1):
                images[(c * chunks + q) * (half - 1) + n].wait()

        def combine(at, carry):
            h = at // (BANDS // step)
            rows = pl.ds(pl.multiple_of(at % (BANDS // step) * step, step), step)
            total = [jnp.zeros((step, chunk), jnp.float32) for _ in range(3)]
            for c in range(2):
                own_at = (me - first_of_half) * share + h
                terms = [(x_own[c], send_ref[c, q, own_at, rows, :])]
                for n in range(half - 1):
                    x_other = x_recv_ref[n, c * 8 : c * 8 + 1, :]
                    terms.append((x_other, recv_ref[c, q, n, h, rows, :]))
                for x_term, image in terms:
                    image = image.astype(jnp.float32)
                    total[0] += image
                    total[1] += x_term * image
                    total[2] += (x_term * x_term) * image
            for k in range(3):
                out_ref[k, h, rows, q * chunk : (q + 1) * chunk] = total[k].astype(jnp.bfloat16)
            return carry

        lax.fori_loop(0, share * (BANDS // step), combine, 0)


def shards(
    vis_values, kernel_u, kernel_v, offset_u, offset_v, block_owner, tile_slot, channel_freq
):
    row_count = lax.axis_size("row")
    freq_count = lax.axis_size("freq")
    blocks = vis_values.shape[1]
    vis_count = vis_values.shape[3]
    taps = kernel_u.shape[2]
    width = GRID // row_count
    tiles_slab = GRID // row_count // TU * TILE_COLS
    vmem = pl.BlockSpec(memory_space=pltpu.VMEM)
    chunk = min(256, width)
    chunks = width // chunk
    others = freq_count // 2 - 1
    share = TU // freq_count
    pairs = row_count // 2
    total_blocks = row_count * blocks

    tile = block_owner[0, :, 0] * tiles_slab + tile_slot[0]
    ids = jnp.stack([tile // TILE_COLS, tile % TILE_COLS]).astype(jnp.float32)
    odd = lax.axis_index("row") % 2
    ids = jnp.concatenate([jnp.where(odd == 0, ids, 0.0), jnp.where(odd == 1, ids, 0.0)], axis=1)
    ids = jnp.pad(ids, ((0, 14), (0, 2 * TV - 2 * blocks)))
    x = jnp.broadcast_to((channel_freq - 1.284) / 0.428, (16, 2 * TV))
    scale = 1.0 / math.sqrt(blocks * row_count * vis_count)
    dma = pltpu.SemaphoreType.DMA
    with jax.named_scope("image"):
        image = pl.pallas_call(
            partial(image_kernel, freq_count, row_count),
            out_shape=jax.ShapeDtypeStruct((3, share, BANDS, width), jnp.bfloat16),
            in_specs=[vmem] * 9 + [pl.BlockSpec(memory_space=pl.ANY)] * 2,
            out_specs=vmem,
            scratch_shapes=[
                pltpu.VMEM((taps, blocks, TV), jnp.float32),
                pltpu.VMEM((taps, blocks, TV), jnp.float32),
                pltpu.VMEM((2 * TU, blocks, TV), jnp.float32),
                pltpu.VMEM((2, row_count, 2, TU * blocks // 2 + 16, 2 * TV), jnp.bfloat16),
                pltpu.VMEM((chunks, 2 * TV, 2 * chunk), jnp.bfloat16),
                pltpu.VMEM((BANDS // 16, TU // 2 * 16, 2 * TU * 16), jnp.bfloat16),
                pltpu.VMEM((2 * BANDS, 2 * total_blocks), jnp.bfloat16),
                pltpu.VMEM((total_blocks, 2 * chunk), jnp.bfloat16),
                pltpu.VMEM((2 * TU, BANDS, chunk), jnp.bfloat16),
                pltpu.VMEM((2, chunks, TU // 2, BANDS, chunk), jnp.bfloat16),
                pltpu.VMEM((2, chunks, others, share, BANDS, chunk), jnp.bfloat16),
                pltpu.VMEM((16, chunk), jnp.float32),
                pltpu.VMEM((others, 16, chunk), jnp.float32),
                dma((2,)),
                dma((2, 2)),
                dma((2, pairs - 1, 2)),
                dma((2, pairs - 1, 2)),
                dma((2, pairs, 2)),
                dma((2, pairs, 2)),
                dma((2, chunks, others)),
                dma((2, chunks, others)),
                dma((others,)),
                dma((others,)),
            ],
            compiler_params=pltpu.CompilerParams(
                vmem_limit_bytes=VMEM_LIMIT, collective_id=0, has_side_effects=True
            ),
        )(
            vis_values,
            kernel_u[0].transpose(1, 0, 2),
            kernel_v[0].transpose(1, 0, 2),
            offset_u,
            offset_v,
            ids,
            x,
            phase_table(chunk),
            band_table(scale),
            tile_tables(row_count, chunk),
            inner_table(),
        )
    return image.reshape(3, GRID // freq_count, width)


def solution(mesh):
    return jax.shard_map(
        shards,
        mesh=mesh,
        in_specs=(
            P("freq", "row", None, None),
            P("freq", "row", None, None),
            P("freq", "row", None, None),
            P("freq", "row", None),
            P("freq", "row", None),
            P("freq", "row", None),
            P("freq", "row"),
            P("freq"),
        ),
        out_specs=P(None, "freq", "row"),
        check_vma=False,
    )
```
